32 devices in a mesh: sib: 2 (over x), row: 4 (over y, core), col: 4 (over z).
Axes of the slice: x: 2, y: 2, z: 4, core: 2. Of those that a mesh axis runs over, the one named last changes fastest.
Arguments:
- child_tiles: float32 [2, 16, 32, 128, 128], P('sib', ('row', 'col')), may hold values from -6 to 6
- child_rows: int32 [2, 64], P('sib'), may hold values from 0 to 127, as said below
- child_slots: int32 [2, 16, 32], P('sib', ('row', 'col')), may hold values from 0 to 4095, as said below
- tile_count: int32 [2, 16], P('sib', ('row', 'col')), may hold values from 16 to 32, as said below
- inverses: float32 [2, 512, 512], replicated, as said below
Outputs:
- factored: float32 [16, 8, 32, 4, 128, 128], P(None, ('sib', 'row'), None, 'col')
The draws below stay inside these ranges and needn't reach their ends.
Inputs may be any that keep to these rules, and one draw needn't show every extreme that they name: `child_rows`: A child's entries are distinct; entry i leaves the same remainder as i when divided by the number of grid rows of the parent. `child_slots`: call the owner of parent tile (I, J) the grid row I mod (number of grid rows) and grid column J mod (number of grid columns). Among the live slots of one device at most 2 carry tiles with one owner; in every draw some device reaches 2 for some owner. `tile_count`: some device of each child has all 32 slots live. `inverses`: each matrix is lower triangular with positive diagonal.
All inputs are finite; a program needn't handle non-finite values.
Results may differ from the reference program's by a relative error of at most 0.00012.
Values sent between devices are 32-bit elements; how exact they have to be, the bound alone decides.
A program may use at most 192 MiB of HBM per device.

```python
import math
import jax
import jax.numpy as jnp
from jax import lax

NF = 16384
TILE = 128
PANEL = 512
NPANEL = 2
CHILD_TILES = 64
CAP = 2
TSLOT = 32
N_SIB = 2
N_ROW = 4
N_COL = 4


def draw_child_rows(key, part):
    key = jax.random.fold_in(key, 11)
    grid = N_SIB * N_ROW
    per_residue = CHILD_TILES // grid
    subkeys = jax.random.split(key, N_SIB * grid)
    shuffled = jax.vmap(lambda k: jax.random.permutation(k, NF // TILE // grid))(subkeys)[:, :per_residue]
    quotient = shuffled.reshape(N_SIB, grid, per_residue).transpose(0, 2, 1)
    residue = jnp.arange(grid, dtype=jnp.int32)
    return (residue[None, None, :] + grid * quotient).reshape(N_SIB, CHILD_TILES).astype(jnp.int32)


def slots_of_device(k):
    grid = N_SIB * N_ROW
    owners_all = grid * N_COL
    pieces = jax.random.split(k, 4)
    owners = jax.random.permutation(pieces[0], owners_all)[:TSLOT // CAP]
    owners = jax.random.permutation(pieces[1], jnp.repeat(owners, CAP))
    owner_row = owners // N_COL
    owner_col = owners % N_COL
    i = owner_row + grid * jax.random.randint(pieces[2], (TSLOT,), 0, CHILD_TILES // grid)
    j = owner_col + N_COL * jax.random.randint(pieces[3], (TSLOT,), 0, CHILD_TILES // N_COL)
    return i * CHILD_TILES + j


def draw_child_slots(key, part):
    key = jax.random.fold_in(key, 12)
    subkeys = jax.random.split(key, N_SIB * N_ROW * N_COL)
    return jax.vmap(slots_of_device)(subkeys).reshape(N_SIB, N_ROW * N_COL, TSLOT).astype(jnp.int32)


def draw_tile_count(key, part):
    key = jax.random.fold_in(key, 13)
    pieces = jax.random.split(key, 2)
    counts = jax.random.randint(pieces[0], (N_SIB, N_ROW * N_COL), TSLOT // 2, TSLOT + 1)
    fullest = jax.random.randint(pieces[1], (N_SIB,), 0, N_ROW * N_COL)
    device_ids = jnp.arange(N_ROW * N_COL, dtype=jnp.int32)
    counts = jnp.where(device_ids[None, :] == fullest[:, None], TSLOT, counts)
    return counts.astype(jnp.int32)


def draw_inverses(key, part):
    key = jax.random.fold_in(key, 14)
    pieces = jax.random.split(key, 2)
    diagonal_part = jnp.exp(jax.random.uniform(pieces[0], (NPANEL, PANEL), jnp.float32, math.log(0.05), math.log(0.2)))
    noise_values = jax.random.normal(pieces[1], (NPANEL, PANEL, PANEL), jnp.float32)
    strict = jnp.tril(jnp.ones((PANEL, PANEL), jnp.float32), -1)
    identity = jnp.eye(PANEL, dtype=jnp.float32)
    result = noise_values * (0.1 / math.sqrt(PANEL)) * strict[None] + diagonal_part[:, :, None] * identity[None]
    return result.astype(jnp.float32)


def shard_levels(stream_key, extent, cuts, least, high):
    factor_of, own = 1.0, jax.random.fold_in(stream_key, 6)
    for position, blocks in cuts:
        steps = jnp.exp(jax.random.uniform(jax.random.fold_in(own, position), (blocks,), jnp.float32, least / len(cuts), high / len(cuts)))
        factor_of = factor_of * jnp.repeat(steps, extent[position] // blocks).reshape([-1 if axis == position else 1 for axis in range(len(extent))])
    return factor_of


def noise(stream_key, dims, deviation, most, cuts=(), kind=jnp.bfloat16):
    factor_of = shard_levels(stream_key, dims, cuts, -0.22, 0.18) if cuts else 1.0
    values = jax.random.normal(stream_key, dims, jnp.float32) * deviation * factor_of
    return jnp.minimum(jnp.maximum(values, -most), most).astype(kind)


def setup_inputs(seed: int = 0) -> dict:
    arg_keys = jax.random.split(jax.random.key(seed), 6)
    return {
        "child_tiles": noise(arg_keys[0], (N_SIB, N_ROW * N_COL, TSLOT, TILE, TILE), 1.0, 6.0, ((0, 2), (1, 16)), jnp.float32),
        "child_rows": draw_child_rows(jax.random.fold_in(arg_keys[5], 71), 0),
        "child_slots": draw_child_slots(jax.random.fold_in(arg_keys[5], 71), 0),
        "tile_count": draw_tile_count(jax.random.fold_in(arg_keys[5], 71), 0),
        "inverses": draw_inverses(jax.random.fold_in(arg_keys[5], 71), 0),
    }


def reference(child_tiles, child_rows, child_slots, tile_count, inverses):
    tile_order = NF // TILE
    grid_rows = N_SIB * N_ROW
    front_tiles = jnp.zeros((tile_order, tile_order, TILE, TILE), jnp.float32)
    for child_index in range(N_SIB):
        tile_data = child_tiles[child_index].reshape(-1, TILE, TILE)
        slot_order = jnp.arange(TSLOT, dtype=jnp.int32)
        is_live = (slot_order[None, :] < tile_count[child_index][:, None]).reshape(-1)
        slot_ids = child_slots[child_index].reshape(-1)
        row_list = child_rows[child_index]
        parent_row = row_list[slot_ids // CHILD_TILES]
        parent_col = row_list[slot_ids % CHILD_TILES]
        weighted = tile_data * is_live.astype(jnp.float32)[:, None, None]
        front_tiles = front_tiles.at[parent_row, parent_col].add(weighted)
    matrix = front_tiles.transpose(0, 2, 1, 3).reshape(NF, NF)
    for panel_step in range(NPANEL):
        start = panel_step * PANEL
        finish = start + PANEL
        factor = jnp.dot(matrix[finish:, start:finish], inverses[panel_step].T, precision=lax.Precision.HIGHEST)
        matrix = matrix.at[finish:, start:finish].set(factor)
        update = jnp.dot(factor, factor.T, precision=lax.Precision.HIGHEST)
        matrix = matrix.at[finish:, finish:].add(-update)
    result_tiles = matrix.reshape(tile_order, TILE, tile_order, TILE).transpose(0, 2, 1, 3)
    return result_tiles.reshape(tile_order // grid_rows, grid_rows, tile_order // N_COL, N_COL, TILE, TILE)
```

```python
import functools

import jax
import jax.numpy as jnp
from jax import lax
from jax.experimental import pallas as pl
from jax.experimental.pallas import tpu as pltpu
from jax.sharding import PartitionSpec as P

NF = 16384
TILE = 128
PANEL = 512
NPANEL = 2
CHILD_TILES = 64
CAP = 2


def broadcast(value, axis, source):
    kept = jnp.where(lax.axis_index(axis) == source, value, 0).astype(value.dtype)
    return lax.psum(kept, axis)


def local(child_tiles, child_rows, child_slots, tile_count, inverses):
    grid_rows = lax.axis_size("sib") * lax.axis_size("row")
    columns = lax.axis_size("col")
    devices = grid_rows * columns
    tile_order = NF // TILE
    local_rows = tile_order // grid_rows
    local_cols = tile_order // columns
    tile_data = child_tiles[0, 0]
    slot_ids = child_slots[0, 0]
    live_count = tile_count[0, 0]
    row_list = child_rows[0]
    slot_total = slot_ids.shape[0]
    child_row = slot_ids // CHILD_TILES
    child_col = slot_ids % CHILD_TILES
    positions = jnp.arange(CHILD_TILES, dtype=jnp.int32)
    parent_row = jnp.sum(
        jnp.where(child_row[:, None] == positions[None, :], row_list[None, :], 0), axis=1
    )
    parent_col = jnp.sum(
        jnp.where(child_col[:, None] == positions[None, :], row_list[None, :], 0), axis=1
    )
    owner_index = parent_row % grid_rows * columns + parent_col % columns
    target = parent_row // grid_rows * local_cols + parent_col // columns
    slot_order = jnp.arange(slot_total, dtype=jnp.int32)
    is_live = slot_order < live_count
    earlier = (
        (owner_index[:, None] == owner_index[None, :])
        & is_live[None, :]
        & (slot_order[None, :] < slot_order[:, None])
    )
    slot_rank = jnp.sum(earlier.astype(jnp.int32), axis=1)
    slot_place = jnp.where(is_live, owner_index * CAP + slot_rank, devices * CAP)
    outgoing = (
        jnp.zeros((devices * CAP, TILE, TILE), jnp.float32)
        .at[slot_place]
        .set(tile_data, mode="drop")
    )
    destined = jnp.zeros((devices * CAP,), jnp.int32).at[slot_place].set(target, mode="drop")
    arrived, landing = (
        lax.all_to_all(
            outgoing.reshape(devices, CAP, TILE, TILE),
            ("sib", "row", "col"),
            split_axis=0,
            concat_axis=0,
            tiled=True,
        ),
        lax.all_to_all(
            destined.reshape(devices, CAP),
            ("sib", "row", "col"),
            split_axis=0,
            concat_axis=0,
            tiled=True,
        ),
    )
    front_tiles = jnp.zeros((local_rows * local_cols, TILE, TILE), jnp.float32)
    front_tiles = front_tiles.at[landing.reshape(-1)].add(arrived.reshape(-1, TILE, TILE))
    front_tiles = front_tiles.reshape(local_rows, local_cols, TILE, TILE)
    my_row = lax.axis_index(("sib", "row"))
    my_col = lax.axis_index("col")
    panel_tiles = PANEL // TILE
    root_count = grid_rows // columns
    tile_ids = jnp.arange(local_rows, dtype=jnp.int32) * grid_rows + my_row
    for panel_step in range(NPANEL):
        first_tile = panel_tiles * panel_step
        below_tile = first_tile + panel_tiles
        column_slot = first_tile // columns
        start_col = first_tile % columns
        is_below = tile_ids >= below_tile
        weights = inverses[panel_step]
        column_block = front_tiles[:, column_slot]
        holds_panel = (my_col >= start_col) & (my_col < start_col + panel_tiles)
        offset = jnp.clip(my_col - start_col, 0, panel_tiles - 1)
        everyone = lax.all_gather(column_block[None], "col", axis=0, tiled=True)
        chosen = everyone[start_col : start_col + panel_tiles]
        panel_rows = chosen.transpose(1, 2, 0, 3).reshape(local_rows * TILE, PANEL)
        factor = jnp.dot(panel_rows, weights.T, precision=lax.Precision.HIGHEST)
        factor = (
            factor.reshape(local_rows, TILE, PANEL) * is_below.astype(jnp.float32)[:, None, None]
        )
        panel_piece = lax.dynamic_slice_in_dim(factor, offset * TILE, TILE, 2)
        replace = is_below[:, None, None] & holds_panel
        front_tiles = front_tiles.at[:, column_slot].set(
            jnp.where(replace, panel_piece, column_block)
        )
        received = [
            broadcast(factor, ("sib", "row"), root_step * columns + my_col)
            for root_step in range(root_count)
        ]
        column_factor = jnp.stack(received, 1).reshape(local_cols, TILE, PANEL)
        front_tiles = front_tiles - jnp.einsum(
            "aip,bjp->abij", factor, column_factor, precision=lax.Precision.HIGHEST
        )
    return front_tiles.reshape(local_rows, 1, local_cols, 1, TILE, TILE)


def route(child_rows, child_slots, tile_count, grid_rows, columns, local_cols):
    slot_ids = child_slots[0, 0]
    row_list = child_rows[0]
    slot_total = slot_ids.shape[0]
    positions = jnp.arange(CHILD_TILES, dtype=jnp.int32)

    def look_up(index):
        return jnp.sum(jnp.where(index[:, None] == positions[None, :], row_list[None, :], 0), axis=1)

    parent_row = look_up(slot_ids // CHILD_TILES)
    parent_col = look_up(slot_ids % CHILD_TILES)
    owner_index = parent_row % grid_rows * columns + parent_col % columns
    target = parent_row // grid_rows * local_cols + parent_col // columns
    slot_order = jnp.arange(slot_total, dtype=jnp.int32)
    is_live = slot_order < tile_count[0, 0]
    earlier = (
        (owner_index[:, None] == owner_index[None, :])
        & is_live[None, :]
        & (slot_order[None, :] < slot_order[:, None])
    )
    slot_rank = jnp.sum(earlier.astype(jnp.int32), axis=1)
    slot_place = jnp.where(is_live, owner_index * CAP + slot_rank, grid_rows * columns * CAP)
    return slot_place, target


def collect_kernel(local_cols, land_ref, tiles_ref, out_ref):
    out_ref[...] = jnp.zeros_like(out_ref)

    def step(n, carry):
        place = land_ref[n] - 1
        b = lax.rem(place, local_cols)

        @pl.when((place >= 0) & (b < NPANEL))
        def _():
            a = place // local_cols
            out_ref[b, a] = out_ref[b, a] + tiles_ref[n]

        return carry

    lax.fori_loop(0, land_ref.shape[0], step, 0)


def exchange_kernel(
    p_ref, s_ref, z_ref,
    own_sem, g_recv, up_send, down_send,
    h_recv, x_send, y_send, core_send, copy_sem,
    z_local, z_send, z_recv,
):
    x = lax.axis_index("sib")
    r = lax.axis_index("row")
    z = lax.axis_index("col")
    last = lax.axis_size("col") - 1
    y, core = r // 2, lax.rem(r, 2)
    right_core = core == lax.rem(z, 2)
    is_source = right_core & (y == z // 2)
    is_relay = right_core & (y != z // 2)
    up, down = (x, r, z + 1), (x, r, z - 1)
    x_peer = (1 - x, r, z)
    y_peer = (x, lax.rem(r + 2, 4), z)
    core_peer = (x, r + 1 - 2 * core, z)
    has_up, has_down = z < last, z > 0

    def remote(src, dst, send, recv, device):
        return pltpu.make_async_remote_copy(
            src_ref=src, dst_ref=dst, send_sem=send, recv_sem=recv,
            device_id=device, device_id_type=pl.DeviceIdType.MESH,
        )

    barrier = pltpu.get_barrier_semaphore()
    for peer in (x_peer, y_peer, core_peer):
        pl.semaphore_signal(barrier, inc=1, device_id=peer, device_id_type=pl.DeviceIdType.MESH)

    @pl.when(has_up)
    def _():
        pl.semaphore_signal(barrier, inc=1, device_id=up, device_id_type=pl.DeviceIdType.MESH)

    @pl.when(has_down)
    def _():
        pl.semaphore_signal(barrier, inc=1, device_id=down, device_id_type=pl.DeviceIdType.MESH)

    pl.semaphore_wait(barrier, 3 + jnp.where(has_up, 1, 0) + jnp.where(has_down, 1, 0))

    def up_copy(src, c, p):
        return remote(src, s_ref.at[0, c, p], up_send.at[c, p], g_recv.at[c, p], up)

    def down_copy(src, c, p):
        return remote(src, s_ref.at[0, c, p], down_send.at[c, p], g_recv.at[c, p], down)

    def own_copy(p):
        return pltpu.make_async_copy(p_ref.at[p], s_ref.at[0, z, p], own_sem.at[p])

    def plane_copies(src, c, p):
        there = s_ref.at[1 + x, c, p]
        recv = h_recv.at[x, c, p]
        return (
            remote(src, there, x_send.at[c, p], recv, x_peer),
            remote(src, there, y_send.at[c, p], recv, y_peer),
            remote(src, there, core_send.at[x, c, p], recv, core_peer),
            pltpu.make_async_copy(src, there, copy_sem.at[c, p]),
        )

    def relay_x(c, p):
        here = s_ref.at[1 + x, c, p]
        return remote(here, here, x_send.at[c, p], h_recv.at[x, c, p], x_peer)

    def to_core(k, c, p):
        here = s_ref.at[1 + k, c, p]
        return remote(here, here, core_send.at[k, c, p], h_recv.at[k, c, p], core_peer)

    def units(t):
        if t == 0:
            return [(z, None, 0)]
        return [(z - t, z >= t, -1), (z + t, z + t <= last, 1)]

    def guarded(condition, body):
        if condition is None:
            body()
        else:
            pl.when(condition)(body)

    def gather_step(p, t):
        for c, exists, side in units(t):
            def body(c=c, side=side):
                if side == 0:
                    src = p_ref.at[p]
                    own_copy(p).start()
                else:
                    src = s_ref.at[0, c, p]
                    up_copy(src, c, p).wait_recv()
                if side <= 0:
                    pl.when(has_up)(lambda: up_copy(src, c, p).start())
                if side >= 0:
                    pl.when(has_down)(lambda: down_copy(src, c, p).start())

                @pl.when(is_source)
                def _():
                    for copy in plane_copies(src, c, p):
                        copy.start()

            guarded(exists, body)

    def relay_step(p, t):
        for c, exists, side in units(t):
            def body(c=c):
                @pl.when(is_relay)
                def _():
                    to_core(x, c, p).wait_recv()
                    relay_x(c, p).start()
                    to_core(x, c, p).start()

                @pl.when(right_core)
                def _():
                    to_core(1 - x, c, p).wait_recv()
                    to_core(1 - x, c, p).start()

            guarded(exists, body)

    def corner_local():
        return pltpu.make_async_copy(s_ref.at[0, :, 0, 0], z_ref.at[r], z_local)

    def corner_x():
        return remote(s_ref.at[0, :, 0, 0], z_ref.at[r], z_send.at[0], z_recv.at[0], x_peer)

    def corner_core():
        return remote(z_ref.at[r], z_ref.at[r], z_send.at[1], z_recv.at[1], core_peer)

    def corner_y():
        pair = z_ref.at[pl.ds(2 * y, 2)]
        return remote(pair, pair, z_send.at[2], z_recv.at[2], y_peer)

    steps = [(p, t) for p in range(NPANEL) for t in range(4)]
    for n, (p, t) in enumerate(steps):
        gather_step(p, t)
        if n:
            relay_step(*steps[n - 1])
        if n == 4:
            own_copy(0).wait()

            @pl.when(x == 1)
            def _():
                corner_local().start()
                corner_x().start()
        if n == 5:
            @pl.when(x == 1)
            def _():
                corner_local().wait()

            @pl.when(x == 0)
            def _():
                corner_x().wait_recv()

            corner_core().start()
        if n == 6:
            corner_core().wait_recv()
            corner_y().start()
    relay_step(*steps[-1])

    own_copy(1).wait()
    corner_y().wait_recv()
    pl.when(x == 1)(lambda: corner_x().wait_send())
    corner_core().wait_send()
    corner_y().wait_send()
    for p, t in steps:
        for c, exists, side in units(t):
            def body(c=c, side=side, p=p):
                src = p_ref.at[p] if side == 0 else s_ref.at[0, c, p]
                if side <= 0:
                    pl.when(has_up)(lambda: up_copy(src, c, p).wait_send())
                if side >= 0:
                    pl.when(has_down)(lambda: down_copy(src, c, p).wait_send())

                @pl.when(is_source)
                def _():
                    first, second, third, here = plane_copies(src, c, p)
                    first.wait_send()
                    second.wait_send()
                    third.wait_send()
                    here.wait()

                @pl.when(is_relay)
                def _():
                    relay_x(c, p).wait_send()
                    to_core(x, c, p).wait_send()

                @pl.when(right_core)
                def _():
                    to_core(1 - x, c, p).wait_send()

                @pl.when(jnp.logical_not(right_core))
                def _():
                    to_core(x, c, p).wait_recv()
                    to_core(1 - x, c, p).wait_recv()

            guarded(exists, body)


def split(value):
    high = value.astype(jnp.bfloat16)
    return high, (value - high.astype(jnp.float32)).astype(jnp.bfloat16)


def dot3(left, right):
    dims = (((1,), (1,)), ((), ()))
    dot = functools.partial(lax.dot_general, dimension_numbers=dims, preferred_element_type=jnp.float32)
    return dot(left[0], right[0]) + (dot(left[0], right[1]) + dot(left[1], right[0]))


def solve_kernel(where_ref, s_ref, z_ref, w_ref, high_ref, low_ref, own_ref, wh, wl, qh, ql, full):
    slab, part = pl.program_id(0), pl.program_id(1)
    rows = s_ref.shape[3]

    @pl.when((slab == 0) & (part == 0))
    def _():
        for p in range(NPANEL):
            wh[p], wl[p] = split(w_ref[p])
        corner = jnp.concatenate([z_ref[:, c].reshape(PANEL, TILE) for c in range(4)], axis=1)
        qh[...], ql[...] = split(dot3(split(corner), (wh[0], wl[0])))

    def columns(p):
        return jnp.concatenate(
            [s_ref[0, c, p].reshape(rows * TILE, TILE) for c in range(4)], axis=1
        )

    a = part * rows + lax.broadcasted_iota(jnp.int32, (rows * TILE, 1), 0) // TILE
    tile_row = a * 8 + where_ref[slab]
    first = dot3(split(columns(0)), (wh[0], wl[0]))
    first_parts = split(first)
    rest = columns(1) - dot3(first_parts, (qh[...], ql[...]))
    second = dot3(split(rest), (wh[1], wl[1]))
    first = jnp.where(tile_row >= 4, first, 0.0)
    second = jnp.where(tile_row >= 8, second, 0.0)
    full[:, :PANEL] = first
    full[:, PANEL:] = second
    high, low = split(full[...])
    high_ref[...] = high.reshape(high_ref.shape)
    low_ref[...] = low.reshape(low_ref.shape)

    @pl.when(slab == 0)
    def _():
        for p in range(NPANEL):
            start = pl.multiple_of(p * PANEL + where_ref[3] * TILE, TILE)
            own_ref[p] = full[:, pl.ds(start, TILE)].reshape(rows, TILE, TILE)


def update_kernel(local_cols, where_ref, land_ref, rh_ref, rl_ref, ch_ref, cl_ref, tiles_ref, own_ref, out_ref):
    step = pl.program_id(0)
    a_total, b_block = out_ref.shape[0], out_ref.shape[1]
    pairs = b_block // 2
    a_block = 4
    depth = rh_ref.shape[-1]

    def chunk(i, carry):
        a0 = i * a_block
        left = tuple(ref[0, pl.ds(a0, a_block)].reshape(a_block * TILE, depth) for ref in (rh_ref, rl_ref))
        for k in range(2):
            right = tuple(ref[k].reshape(pairs * TILE, depth) for ref in (ch_ref, cl_ref))
            product = -dot3(left, right)
            for m in range(pairs):
                out_ref[pl.ds(a0, a_block), 2 * m + k] = product[:, m * TILE : (m + 1) * TILE].reshape(
                    a_block, TILE, TILE
                )
        return carry

    lax.fori_loop(0, a_total // a_block, chunk, 0)

    def add(n, carry):
        place = land_ref[n] - 1
        b = lax.rem(place, local_cols) - step * b_block

        @pl.when((place >= 0) & (b >= 0) & (b < b_block))
        def _():
            a = place // local_cols
            out_ref[a, b] = out_ref[a, b] + tiles_ref[n]

        return carry

    lax.fori_loop(0, land_ref.shape[0], add, 0)

    @pl.when(step == 0)
    def _():
        for p in range(NPANEL):
            @pl.when(where_ref[0] >= (p + 1) * 4)
            def _():
                out_ref[0, p] = own_ref[p, 0]

            out_ref[1:, p] = own_ref[p, 1:]


def local_fast(child_tiles, child_rows, child_slots, tile_count, inverses):
    grid_rows = lax.axis_size("sib") * lax.axis_size("row")
    columns = lax.axis_size("col")
    devices = grid_rows * columns
    tile_order = NF // TILE
    local_rows = tile_order // grid_rows
    local_cols = tile_order // columns
    axes = ("sib", "row", "col")
    slot_place, target = route(child_rows, child_slots, tile_count, grid_rows, columns, local_cols)
    outgoing = (
        jnp.zeros((devices * CAP, TILE, TILE), jnp.float32)
        .at[slot_place]
        .set(child_tiles[0, 0], mode="drop")
    )
    destined = jnp.zeros((devices * CAP,), jnp.int32).at[slot_place].set(target + 1, mode="drop")
    arrived = lax.all_to_all(
        outgoing.reshape(devices, CAP, TILE, TILE), axes, split_axis=0, concat_axis=0, tiled=True
    ).reshape(devices * CAP, TILE, TILE)
    landing = lax.all_to_all(
        destined.reshape(devices, CAP), axes, split_axis=0, concat_axis=0, tiled=True
    ).reshape(devices * CAP)

    vmem = pl.BlockSpec(memory_space=pltpu.VMEM)
    smem = pl.BlockSpec(memory_space=pltpu.SMEM)
    anywhere = pl.BlockSpec(memory_space=pl.ANY)
    panels = pl.pallas_call(
        functools.partial(collect_kernel, local_cols),
        out_shape=jax.ShapeDtypeStruct((NPANEL, local_rows, TILE, TILE), jnp.float32),
        in_specs=[smem, vmem],
        out_specs=vmem,
        compiler_params=pltpu.CompilerParams(vmem_limit_bytes=24 * 2**20),
        name="collect",
    )(landing, arrived)

    dma = pltpu.SemaphoreType.DMA
    unit = (columns, NPANEL)
    slabs, corner = pl.pallas_call(
        exchange_kernel,
        out_shape=(
            jax.ShapeDtypeStruct((3, columns, NPANEL, local_rows, TILE, TILE), jnp.float32),
            jax.ShapeDtypeStruct((4, columns, TILE, TILE), jnp.float32),
        ),
        in_specs=[anywhere],
        out_specs=(anywhere, anywhere),
        scratch_shapes=[
            dma((NPANEL,)), dma(unit), dma(unit), dma(unit),
            dma((2,) + unit), dma(unit), dma(unit), dma((2,) + unit), dma(unit),
            dma, dma((3,)), dma((3,)),
        ],
        compiler_params=pltpu.CompilerParams(collective_id=0, has_side_effects=True),
        name="exchange",
    )(panels)

    my_row = lax.axis_index(("sib", "row"))
    my_col = lax.axis_index("col")
    where = jnp.stack([my_row, my_col, my_col + 4, my_col]).astype(jnp.int32)
    rows = 4
    order = NPANEL * PANEL
    factor_shape = jax.ShapeDtypeStruct((3, local_rows, TILE, order), jnp.bfloat16)
    factor_spec = pl.BlockSpec((1, rows, TILE, order), lambda s, i, w: (s, i, 0, 0))
    parts = local_rows // rows
    high, low, own = pl.pallas_call(
        solve_kernel,
        grid_spec=pltpu.PrefetchScalarGridSpec(
            num_scalar_prefetch=1,
            grid=(3, parts),
            in_specs=[
                pl.BlockSpec((1, columns, NPANEL, rows, TILE, TILE), lambda s, i, w: (s, 0, 0, i, 0, 0)),
                pl.BlockSpec((4, columns, TILE, TILE), lambda s, i, w: (0, 0, 0, 0)),
                pl.BlockSpec((NPANEL, PANEL, PANEL), lambda s, i, w: (0, 0, 0)),
            ],
            out_specs=(
                factor_spec,
                factor_spec,
                pl.BlockSpec(
                    (NPANEL, rows, TILE, TILE),
                    lambda s, i, w: (0, jnp.where(s == 0, i, parts - 1), 0, 0),
                ),
            ),
            scratch_shapes=[
                pltpu.VMEM((NPANEL, PANEL, PANEL), jnp.bfloat16),
                pltpu.VMEM((NPANEL, PANEL, PANEL), jnp.bfloat16),
                pltpu.VMEM((PANEL, PANEL), jnp.bfloat16),
                pltpu.VMEM((PANEL, PANEL), jnp.bfloat16),
                pltpu.VMEM((rows * TILE, order), jnp.float32),
            ],
        ),
        out_shape=(
            factor_shape,
            factor_shape,
            jax.ShapeDtypeStruct((NPANEL, local_rows, TILE, TILE), jnp.float32),
        ),
        compiler_params=pltpu.CompilerParams(vmem_limit_bytes=48 * 2**20),
        name="solve",
    )(where, slabs, corner, inverses)

    b_block = 4
    row_spec = pl.BlockSpec((1, local_rows, TILE, order), lambda j, w, l: (0, 0, 0, 0))
    col_spec = pl.BlockSpec((pl.Element(2), pl.Element(b_block // 2), pl.Element(TILE), pl.Element(order)),
                            lambda j, w, l: (1, j * (b_block // 2), 0, 0))
    front = pl.pallas_call(
        functools.partial(update_kernel, local_cols),
        grid_spec=pltpu.PrefetchScalarGridSpec(
            num_scalar_prefetch=2,
            grid=(local_cols // b_block,),
            in_specs=[
                row_spec, row_spec, col_spec, col_spec,
                pl.BlockSpec((devices * CAP, TILE, TILE), lambda j, w, l: (0, 0, 0)),
                pl.BlockSpec((NPANEL, local_rows, TILE, TILE), lambda j, w, l: (0, 0, 0, 0)),
            ],
            out_specs=pl.BlockSpec((local_rows, b_block, TILE, TILE), lambda j, w, l: (0, j, 0, 0)),
        ),
        out_shape=jax.ShapeDtypeStruct((local_rows, local_cols, TILE, TILE), jnp.float32),
        compiler_params=pltpu.CompilerParams(vmem_limit_bytes=56 * 2**20),
        name="update",
    )(where, landing, high, low, high, low, arrived, own)
    return front.reshape(local_rows, 1, local_cols, 1, TILE, TILE)


def solution(mesh):
    sizes = (mesh.shape["sib"], mesh.shape["row"], mesh.shape["col"])
    return jax.shard_map(
        local_fast if sizes == (2, 4, 4) else local,
        mesh=mesh,
        in_specs=(
            P("sib", ("row", "col"), None, None, None),
            P("sib", None),
            P("sib", ("row", "col"), None),
            P("sib", ("row", "col")),
            P(),
        ),
        out_specs=P(None, ("sib", "row"), None, "col", None, None),
        check_vma=False,
    )
```

```python
import functools

import jax
import jax.numpy as jnp
from jax import lax
from jax.experimental import pallas as pl
from jax.experimental.pallas import tpu as pltpu
from jax.sharding import PartitionSpec as P

NF = 16384
TILE = 128
PANEL = 512
NPANEL = 2
CHILD_TILES = 64
CAP = 2


def broadcast(value, axis, source):
    kept = jnp.where(lax.axis_index(axis) == source, value, 0).astype(value.dtype)
    return lax.psum(kept, axis)


def local(child_tiles, child_rows, child_slots, tile_count, inverses):
    grid_rows = lax.axis_size("sib") * lax.axis_size("row")
    columns = lax.axis_size("col")
    devices = grid_rows * columns
    tile_order = NF // TILE
    local_rows = tile_order // grid_rows
    local_cols = tile_order // columns
    tile_data = child_tiles[0, 0]
    slot_ids = child_slots[0, 0]
    live_count = tile_count[0, 0]
    row_list = child_rows[0]
    slot_total = slot_ids.shape[0]
    child_row = slot_ids // CHILD_TILES
    child_col = slot_ids % CHILD_TILES
    positions = jnp.arange(CHILD_TILES, dtype=jnp.int32)
    parent_row = jnp.sum(
        jnp.where(child_row[:, None] == positions[None, :], row_list[None, :], 0), axis=1
    )
    parent_col = jnp.sum(
        jnp.where(child_col[:, None] == positions[None, :], row_list[None, :], 0), axis=1
    )
    owner_index = parent_row % grid_rows * columns + parent_col % columns
    target = parent_row // grid_rows * local_cols + parent_col // columns
    slot_order = jnp.arange(slot_total, dtype=jnp.int32)
    is_live = slot_order < live_count
    earlier = (
        (owner_index[:, None] == owner_index[None, :])
        & is_live[None, :]
        & (slot_order[None, :] < slot_order[:, None])
    )
    slot_rank = jnp.sum(earlier.astype(jnp.int32), axis=1)
    slot_place = jnp.where(is_live, owner_index * CAP + slot_rank, devices * CAP)
    outgoing = (
        jnp.zeros((devices * CAP, TILE, TILE), jnp.float32)
        .at[slot_place]
        .set(tile_data, mode="drop")
    )
    destined = jnp.zeros((devices * CAP,), jnp.int32).at[slot_place].set(target, mode="drop")
    arrived, landing = (
        lax.all_to_all(
            outgoing.reshape(devices, CAP, TILE, TILE),
            ("sib", "row", "col"),
            split_axis=0,
            concat_axis=0,
            tiled=True,
        ),
        lax.all_to_all(
            destined.reshape(devices, CAP),
            ("sib", "row", "col"),
            split_axis=0,
            concat_axis=0,
            tiled=True,
        ),
    )
    front_tiles = jnp.zeros((local_rows * local_cols, TILE, TILE), jnp.float32)
    front_tiles = front_tiles.at[landing.reshape(-1)].add(arrived.reshape(-1, TILE, TILE))
    front_tiles = front_tiles.reshape(local_rows, local_cols, TILE, TILE)
    my_row = lax.axis_index(("sib", "row"))
    my_col = lax.axis_index("col")
    panel_tiles = PANEL // TILE
    root_count = grid_rows // columns
    tile_ids = jnp.arange(local_rows, dtype=jnp.int32) * grid_rows + my_row
    for panel_step in range(NPANEL):
        first_tile = panel_tiles * panel_step
        below_tile = first_tile + panel_tiles
        column_slot = first_tile // columns
        start_col = first_tile % columns
        is_below = tile_ids >= below_tile
        weights = inverses[panel_step]
        column_block = front_tiles[:, column_slot]
        holds_panel = (my_col >= start_col) & (my_col < start_col + panel_tiles)
        offset = jnp.clip(my_col - start_col, 0, panel_tiles - 1)
        everyone = lax.all_gather(column_block[None], "col", axis=0, tiled=True)
        chosen = everyone[start_col : start_col + panel_tiles]
        panel_rows = chosen.transpose(1, 2, 0, 3).reshape(local_rows * TILE, PANEL)
        factor = jnp.dot(panel_rows, weights.T, precision=lax.Precision.HIGHEST)
        factor = (
            factor.reshape(local_rows, TILE, PANEL) * is_below.astype(jnp.float32)[:, None, None]
        )
        panel_piece = lax.dynamic_slice_in_dim(factor, offset * TILE, TILE, 2)
        replace = is_below[:, None, None] & holds_panel
        front_tiles = front_tiles.at[:, column_slot].set(
            jnp.where(replace, panel_piece, column_block)
        )
        received = [
            broadcast(factor, ("sib", "row"), root_step * columns + my_col)
            for root_step in range(root_count)
        ]
        column_factor = jnp.stack(received, 1).reshape(local_cols, TILE, PANEL)
        front_tiles = front_tiles - jnp.einsum(
            "aip,bjp->abij", factor, column_factor, precision=lax.Precision.HIGHEST
        )
    return front_tiles.reshape(local_rows, 1, local_cols, 1, TILE, TILE)


def route(child_rows, child_slots, tile_count, grid_rows, columns, local_cols):
    slot_ids = child_slots[0, 0]
    row_list = child_rows[0]
    slot_total = slot_ids.shape[0]
    positions = jnp.arange(CHILD_TILES, dtype=jnp.int32)

    def look_up(index):
        return jnp.sum(jnp.where(index[:, None] == positions[None, :], row_list[None, :], 0), axis=1)

    parent_row = look_up(slot_ids // CHILD_TILES)
    parent_col = look_up(slot_ids % CHILD_TILES)
    owner_index = parent_row % grid_rows * columns + parent_col % columns
    target = parent_row // grid_rows * local_cols + parent_col // columns
    slot_order = jnp.arange(slot_total, dtype=jnp.int32)
    is_live = slot_order < tile_count[0, 0]
    earlier = (
        (owner_index[:, None] == owner_index[None, :])
        & is_live[None, :]
        & (slot_order[None, :] < slot_order[:, None])
    )
    slot_rank = jnp.sum(earlier.astype(jnp.int32), axis=1)
    slot_place = jnp.where(is_live, owner_index * CAP + slot_rank, grid_rows * columns * CAP)
    return slot_place, target


def collect_kernel(local_cols, land_ref, tiles_ref, out_ref):
    out_ref[...] = jnp.zeros_like(out_ref)

    def step(n, carry):
        place = land_ref[n] - 1
        b = lax.rem(place, local_cols)

        @pl.when((place >= 0) & (b < NPANEL))
        def _():
            a = place // local_cols
            out_ref[b, a] = out_ref[b, a] + tiles_ref[n]

        return carry

    lax.fori_loop(0, land_ref.shape[0], step, 0)


def exchange_kernel(
    p_ref, s_ref, z_ref,
    g_recv, up_send, down_send,
    h_recv, x_send, y_send, core_send,
    z_send, z_recv,
):
    x = lax.axis_index("sib")
    r = lax.axis_index("row")
    z = lax.axis_index("col")
    last = lax.axis_size("col") - 1
    y, core = r // 2, lax.rem(r, 2)
    right_core = core == lax.rem(z, 2)
    is_source = right_core & (y == z // 2)
    is_relay = right_core & (y != z // 2)
    up, down = (x, r, z + 1), (x, r, z - 1)
    x_peer = (1 - x, r, z)
    y_peer = (x, lax.rem(r + 2, 4), z)
    core_peer = (x, r + 1 - 2 * core, z)
    has_up, has_down = z < last, z > 0

    def remote(src, dst, send, recv, device):
        return pltpu.make_async_remote_copy(
            src_ref=src, dst_ref=dst, send_sem=send, recv_sem=recv,
            device_id=device, device_id_type=pl.DeviceIdType.MESH,
        )

    barrier = pltpu.get_barrier_semaphore()
    for peer in (x_peer, y_peer, core_peer):
        pl.semaphore_signal(barrier, inc=1, device_id=peer, device_id_type=pl.DeviceIdType.MESH)

    @pl.when(has_up)
    def _():
        pl.semaphore_signal(barrier, inc=1, device_id=up, device_id_type=pl.DeviceIdType.MESH)

    @pl.when(has_down)
    def _():
        pl.semaphore_signal(barrier, inc=1, device_id=down, device_id_type=pl.DeviceIdType.MESH)

    pl.semaphore_wait(barrier, 3 + jnp.where(has_up, 1, 0) + jnp.where(has_down, 1, 0))

    def up_copy(src, c, p):
        return remote(src, s_ref.at[0, c, p], up_send.at[c, p], g_recv.at[c, p], up)

    def down_copy(src, c, p):
        return remote(src, s_ref.at[0, c, p], down_send.at[c, p], g_recv.at[c, p], down)

    def plane_copies(src, c, p):
        there = s_ref.at[1 + x, c, p]
        recv = h_recv.at[x, c, p]
        return (
            remote(src, there, x_send.at[c, p], recv, x_peer),
            remote(src, there, y_send.at[c, p], recv, y_peer),
            remote(src, there, core_send.at[x, c, p], recv, core_peer),
        )

    def relay_x(c, p):
        here = s_ref.at[1 + x, c, p]
        return remote(here, here, x_send.at[c, p], h_recv.at[x, c, p], x_peer)

    def to_core(k, c, p):
        here = s_ref.at[1 + k, c, p]
        return remote(here, here, core_send.at[k, c, p], h_recv.at[k, c, p], core_peer)

    def units(t):
        if t == 0:
            return [(z, None, 0)]
        return [(z - t, z >= t, -1), (z + t, z + t <= last, 1)]

    def guarded(condition, body):
        if condition is None:
            body()
        else:
            pl.when(condition)(body)

    def gather_step(p, t):
        for c, exists, side in units(t):
            def body(c=c, side=side):
                if side == 0:
                    src = p_ref.at[p]
                else:
                    src = s_ref.at[0, c, p]
                    up_copy(src, c, p).wait_recv()
                if side <= 0:
                    pl.when(has_up)(lambda: up_copy(src, c, p).start())
                if side >= 0:
                    pl.when(has_down)(lambda: down_copy(src, c, p).start())

                @pl.when(is_source)
                def _():
                    for copy in plane_copies(src, c, p):
                        copy.start()

                if side == 0:
                    s_ref[0, z, p] = p_ref[p]

            guarded(exists, body)

    def relay_step(p, t):
        for c, exists, side in units(t):
            def body(c=c):
                @pl.when(is_relay)
                def _():
                    to_core(x, c, p).wait_recv()
                    relay_x(c, p).start()
                    to_core(x, c, p).start()

                @pl.when(right_core)
                def _():
                    to_core(1 - x, c, p).wait_recv()
                    to_core(1 - x, c, p).start()

            guarded(exists, body)

    def corner_x():
        return remote(s_ref.at[0, :, 0, 0], z_ref.at[r], z_send.at[0], z_recv.at[0], x_peer)

    def corner_core():
        return remote(z_ref.at[r], z_ref.at[r], z_send.at[1], z_recv.at[1], core_peer)

    def corner_y():
        pair = z_ref.at[pl.ds(2 * y, 2)]
        return remote(pair, pair, z_send.at[2], z_recv.at[2], y_peer)

    steps = [(p, t) for p in range(NPANEL) for t in range(4)]
    for n, (p, t) in enumerate(steps):
        gather_step(p, t)
        if n:
            relay_step(*steps[n - 1])
        if n == 4:
            @pl.when(x == 1)
            def _():
                corner_x().start()
                z_ref[r] = s_ref[0, :, 0, 0]
        if n == 5:
            @pl.when(x == 0)
            def _():
                corner_x().wait_recv()

            corner_core().start()
        if n == 6:
            corner_core().wait_recv()
            corner_y().start()
    relay_step(*steps[-1])

    corner_y().wait_recv()
    pl.when(x == 1)(lambda: corner_x().wait_send())
    corner_core().wait_send()
    corner_y().wait_send()
    for p, t in steps:
        for c, exists, side in units(t):
            def body(c=c, side=side, p=p):
                src = p_ref.at[p] if side == 0 else s_ref.at[0, c, p]
                if side <= 0:
                    pl.when(has_up)(lambda: up_copy(src, c, p).wait_send())
                if side >= 0:
                    pl.when(has_down)(lambda: down_copy(src, c, p).wait_send())

                @pl.when(is_source)
                def _():
                    for copy in plane_copies(src, c, p):
                        copy.wait_send()

                @pl.when(is_relay)
                def _():
                    relay_x(c, p).wait_send()
                    to_core(x, c, p).wait_send()

                @pl.when(right_core)
                def _():
                    to_core(1 - x, c, p).wait_send()

                @pl.when(jnp.logical_not(right_core))
                def _():
                    to_core(x, c, p).wait_recv()
                    to_core(1 - x, c, p).wait_recv()

            guarded(exists, body)


def split(value):
    high = value.astype(jnp.bfloat16)
    return high, (value - high.astype(jnp.float32)).astype(jnp.bfloat16)


def dot3(left, right):
    dims = (((1,), (1,)), ((), ()))
    dot = functools.partial(lax.dot_general, dimension_numbers=dims, preferred_element_type=jnp.float32)
    return dot(left[0], right[0]) + (dot(left[0], right[1]) + dot(left[1], right[0]))


def solve_kernel(where_ref, s_ref, z_ref, w_ref, high_ref, low_ref, own_ref, wh, wl, qh, ql, full):
    slab, part = pl.program_id(0), pl.program_id(1)
    rows = s_ref.shape[3]

    @pl.when((slab == 0) & (part == 0))
    def _():
        for p in range(NPANEL):
            wh[p], wl[p] = split(w_ref[p])
        corner = jnp.concatenate([z_ref[:, c].reshape(PANEL, TILE) for c in range(4)], axis=1)
        qh[...], ql[...] = split(dot3(split(corner), (wh[0], wl[0])))

    def columns(p):
        return jnp.concatenate(
            [s_ref[0, c, p].reshape(rows * TILE, TILE) for c in range(4)], axis=1
        )

    a = part * rows + lax.broadcasted_iota(jnp.int32, (rows * TILE, 1), 0) // TILE
    tile_row = a * 8 + where_ref[slab]
    first = dot3(split(columns(0)), (wh[0], wl[0]))
    first_parts = split(first)
    rest = columns(1) - dot3(first_parts, (qh[...], ql[...]))
    second = dot3(split(rest), (wh[1], wl[1]))
    first = jnp.where(tile_row >= 4, first, 0.0)
    second = jnp.where(tile_row >= 8, second, 0.0)
    full[:, :PANEL] = first
    full[:, PANEL:] = second
    high, low = split(full[...])
    high_ref[...] = high.reshape(high_ref.shape)
    low_ref[...] = low.reshape(low_ref.shape)

    @pl.when(slab == 0)
    def _():
        for p in range(NPANEL):
            start = pl.multiple_of(p * PANEL + where_ref[3] * TILE, TILE)
            own_ref[p] = full[:, pl.ds(start, TILE)].reshape(rows, TILE, TILE)


def update_kernel(local_cols, where_ref, land_ref, rh_ref, rl_ref, ch_ref, cl_ref, tiles_ref, own_ref, out_ref):
    step = pl.program_id(0)
    a_total, b_block = out_ref.shape[0], out_ref.shape[1]
    pairs = b_block // 2
    a_block = 4
    depth = rh_ref.shape[-1]

    def chunk(i, carry):
        a0 = i * a_block
        left = tuple(ref[0, pl.ds(a0, a_block)].reshape(a_block * TILE, depth) for ref in (rh_ref, rl_ref))
        for k in range(2):
            right = tuple(ref[k].reshape(pairs * TILE, depth) for ref in (ch_ref, cl_ref))
            product = -dot3(left, right)
            for m in range(pairs):
                out_ref[pl.ds(a0, a_block), 2 * m + k] = product[:, m * TILE : (m + 1) * TILE].reshape(
                    a_block, TILE, TILE
                )
        return carry

    lax.fori_loop(0, a_total // a_block, chunk, 0)

    def add(n, carry):
        place = land_ref[n] - 1
        b = lax.rem(place, local_cols) - step * b_block

        @pl.when((place >= 0) & (b >= 0) & (b < b_block))
        def _():
            a = place // local_cols
            out_ref[a, b] = out_ref[a, b] + tiles_ref[n]

        return carry

    lax.fori_loop(0, land_ref.shape[0], add, 0)

    @pl.when(step == 0)
    def _():
        for p in range(NPANEL):
            @pl.when(where_ref[0] >= (p + 1) * 4)
            def _():
                out_ref[0, p] = own_ref[p, 0]

            out_ref[1:, p] = own_ref[p, 1:]


def local_fast(child_tiles, child_rows, child_slots, tile_count, inverses):
    grid_rows = lax.axis_size("sib") * lax.axis_size("row")
    columns = lax.axis_size("col")
    devices = grid_rows * columns
    tile_order = NF // TILE
    local_rows = tile_order // grid_rows
    local_cols = tile_order // columns
    axes = ("sib", "row", "col")
    slot_place, target = route(child_rows, child_slots, tile_count, grid_rows, columns, local_cols)
    outgoing = (
        jnp.zeros((devices * CAP, TILE, TILE), jnp.float32)
        .at[slot_place]
        .set(child_tiles[0, 0], mode="drop")
    )
    destined = jnp.zeros((devices * CAP,), jnp.int32).at[slot_place].set(target + 1, mode="drop")
    arrived = lax.all_to_all(
        outgoing.reshape(devices, CAP, TILE, TILE), axes, split_axis=0, concat_axis=0, tiled=True
    ).reshape(devices * CAP, TILE, TILE)
    landing = lax.all_to_all(
        destined.reshape(devices, CAP), axes, split_axis=0, concat_axis=0, tiled=True
    ).reshape(devices * CAP)

    vmem = pl.BlockSpec(memory_space=pltpu.VMEM)
    smem = pl.BlockSpec(memory_space=pltpu.SMEM)
    panels = pl.pallas_call(
        functools.partial(collect_kernel, local_cols),
        out_shape=jax.ShapeDtypeStruct((NPANEL, local_rows, TILE, TILE), jnp.float32),
        in_specs=[smem, vmem],
        out_specs=vmem,
        compiler_params=pltpu.CompilerParams(vmem_limit_bytes=24 * 2**20),
        name="collect",
    )(landing, arrived)

    dma = pltpu.SemaphoreType.DMA
    unit = (columns, NPANEL)
    slabs, corner = pl.pallas_call(
        exchange_kernel,
        out_shape=(
            jax.ShapeDtypeStruct((3, columns, NPANEL, local_rows, TILE, TILE), jnp.float32),
            jax.ShapeDtypeStruct((4, columns, TILE, TILE), jnp.float32),
        ),
        in_specs=[vmem],
        out_specs=(vmem, vmem),
        scratch_shapes=[
            dma(unit), dma(unit), dma(unit),
            dma((2,) + unit), dma(unit), dma(unit), dma((2,) + unit),
            dma((3,)), dma((3,)),
        ],
        compiler_params=pltpu.CompilerParams(
            collective_id=0, has_side_effects=True, vmem_limit_bytes=40 * 2**20
        ),
        name="exchange",
    )(panels)

    my_row = lax.axis_index(("sib", "row"))
    my_col = lax.axis_index("col")
    my_sib = lax.axis_index("sib")
    is_source = lax.axis_index("row") == my_col
    picks = [jnp.where(is_source & (my_sib == k), 0, 1 + k) for k in range(2)]
    where = jnp.stack([my_row, my_col, my_col + 4, my_col, 0 * my_col, *picks]).astype(jnp.int32)
    rows = 4
    order = NPANEL * PANEL
    factor_shape = jax.ShapeDtypeStruct((3, local_rows, TILE, order), jnp.bfloat16)
    factor_spec = pl.BlockSpec((1, rows, TILE, order), lambda s, i, w: (s, i, 0, 0))
    parts = local_rows // rows
    high, low, own = pl.pallas_call(
        solve_kernel,
        grid_spec=pltpu.PrefetchScalarGridSpec(
            num_scalar_prefetch=1,
            grid=(3, parts),
            in_specs=[
                pl.BlockSpec((1, columns, NPANEL, rows, TILE, TILE), lambda s, i, w: (w[4 + s], 0, 0, i, 0, 0)),
                pl.BlockSpec((4, columns, TILE, TILE), lambda s, i, w: (0, 0, 0, 0)),
                pl.BlockSpec((NPANEL, PANEL, PANEL), lambda s, i, w: (0, 0, 0)),
            ],
            out_specs=(
                factor_spec,
                factor_spec,
                pl.BlockSpec(
                    (NPANEL, rows, TILE, TILE),
                    lambda s, i, w: (0, jnp.where(s == 0, i, parts - 1), 0, 0),
                ),
            ),
            scratch_shapes=[
                pltpu.VMEM((NPANEL, PANEL, PANEL), jnp.bfloat16),
                pltpu.VMEM((NPANEL, PANEL, PANEL), jnp.bfloat16),
                pltpu.VMEM((PANEL, PANEL), jnp.bfloat16),
                pltpu.VMEM((PANEL, PANEL), jnp.bfloat16),
                pltpu.VMEM((rows * TILE, order), jnp.float32),
            ],
        ),
        out_shape=(
            factor_shape,
            factor_shape,
            jax.ShapeDtypeStruct((NPANEL, local_rows, TILE, TILE), jnp.float32),
        ),
        compiler_params=pltpu.CompilerParams(vmem_limit_bytes=48 * 2**20),
        name="solve",
    )(where, slabs, corner, inverses)

    b_block = 4
    row_spec = pl.BlockSpec((1, local_rows, TILE, order), lambda j, w, l: (0, 0, 0, 0))
    col_spec = pl.BlockSpec((pl.Element(2), pl.Element(b_block // 2), pl.Element(TILE), pl.Element(order)),
                            lambda j, w, l: (1, j * (b_block // 2), 0, 0))
    front = pl.pallas_call(
        functools.partial(update_kernel, local_cols),
        grid_spec=pltpu.PrefetchScalarGridSpec(
            num_scalar_prefetch=2,
            grid=(local_cols // b_block,),
            in_specs=[
                row_spec, row_spec, col_spec, col_spec,
                pl.BlockSpec((devices * CAP, TILE, TILE), lambda j, w, l: (0, 0, 0)),
                pl.BlockSpec((NPANEL, local_rows, TILE, TILE), lambda j, w, l: (0, 0, 0, 0)),
            ],
            out_specs=pl.BlockSpec((local_rows, b_block, TILE, TILE), lambda j, w, l: (0, j, 0, 0)),
        ),
        out_shape=jax.ShapeDtypeStruct((local_rows, local_cols, TILE, TILE), jnp.float32),
        compiler_params=pltpu.CompilerParams(vmem_limit_bytes=56 * 2**20),
        name="update",
    )(where, landing, high, low, high, low, arrived, own)
    return front.reshape(local_rows, 1, local_cols, 1, TILE, TILE)


def solution(mesh):
    sizes = (mesh.shape["sib"], mesh.shape["row"], mesh.shape["col"])
    return jax.shard_map(
        local_fast if sizes == (2, 4, 4) else local,
        mesh=mesh,
        in_specs=(
            P("sib", ("row", "col"), None, None, None),
            P("sib", None),
            P("sib", ("row", "col"), None),
            P("sib", ("row", "col")),
            P(),
        ),
        out_specs=P(None, ("sib", "row"), None, "col", None, None),
        check_vma=False,
    )
```

```python
import functools

import jax
import jax.numpy as jnp
from jax import lax
from jax.experimental import pallas as pl
from jax.experimental.pallas import tpu as pltpu
from jax.sharding import PartitionSpec as P

NF = 16384
TILE = 128
PANEL = 512
NPANEL = 2
CHILD_TILES = 64
CAP = 2


def broadcast(value, axis, source):
    kept = jnp.where(lax.axis_index(axis) == source, value, 0).astype(value.dtype)
    return lax.psum(kept, axis)


def local(child_tiles, child_rows, child_slots, tile_count, inverses):
    grid_rows = lax.axis_size("sib") * lax.axis_size("row")
    columns = lax.axis_size("col")
    devices = grid_rows * columns
    tile_order = NF // TILE
    local_rows = tile_order // grid_rows
    local_cols = tile_order // columns
    tile_data = child_tiles[0, 0]
    slot_ids = child_slots[0, 0]
    live_count = tile_count[0, 0]
    row_list = child_rows[0]
    slot_total = slot_ids.shape[0]
    child_row = slot_ids // CHILD_TILES
    child_col = slot_ids % CHILD_TILES
    positions = jnp.arange(CHILD_TILES, dtype=jnp.int32)
    parent_row = jnp.sum(
        jnp.where(child_row[:, None] == positions[None, :], row_list[None, :], 0), axis=1
    )
    parent_col = jnp.sum(
        jnp.where(child_col[:, None] == positions[None, :], row_list[None, :], 0), axis=1
    )
    owner_index = parent_row % grid_rows * columns + parent_col % columns
    target = parent_row // grid_rows * local_cols + parent_col // columns
    slot_order = jnp.arange(slot_total, dtype=jnp.int32)
    is_live = slot_order < live_count
    earlier = (
        (owner_index[:, None] == owner_index[None, :])
        & is_live[None, :]
        & (slot_order[None, :] < slot_order[:, None])
    )
    slot_rank = jnp.sum(earlier.astype(jnp.int32), axis=1)
    slot_place = jnp.where(is_live, owner_index * CAP + slot_rank, devices * CAP)
    outgoing = (
        jnp.zeros((devices * CAP, TILE, TILE), jnp.float32)
        .at[slot_place]
        .set(tile_data, mode="drop")
    )
    destined = jnp.zeros((devices * CAP,), jnp.int32).at[slot_place].set(target, mode="drop")
    arrived, landing = (
        lax.all_to_all(
            outgoing.reshape(devices, CAP, TILE, TILE),
            ("sib", "row", "col"),
            split_axis=0,
            concat_axis=0,
            tiled=True,
        ),
        lax.all_to_all(
            destined.reshape(devices, CAP),
            ("sib", "row", "col"),
            split_axis=0,
            concat_axis=0,
            tiled=True,
        ),
    )
    front_tiles = jnp.zeros((local_rows * local_cols, TILE, TILE), jnp.float32)
    front_tiles = front_tiles.at[landing.reshape(-1)].add(arrived.reshape(-1, TILE, TILE))
    front_tiles = front_tiles.reshape(local_rows, local_cols, TILE, TILE)
    my_row = lax.axis_index(("sib", "row"))
    my_col = lax.axis_index("col")
    panel_tiles = PANEL // TILE
    root_count = grid_rows // columns
    tile_ids = jnp.arange(local_rows, dtype=jnp.int32) * grid_rows + my_row
    for panel_step in range(NPANEL):
        first_tile = panel_tiles * panel_step
        below_tile = first_tile + panel_tiles
        column_slot = first_tile // columns
        start_col = first_tile % columns
        is_below = tile_ids >= below_tile
        weights = inverses[panel_step]
        column_block = front_tiles[:, column_slot]
        holds_panel = (my_col >= start_col) & (my_col < start_col + panel_tiles)
        offset = jnp.clip(my_col - start_col, 0, panel_tiles - 1)
        everyone = lax.all_gather(column_block[None], "col", axis=0, tiled=True)
        chosen = everyone[start_col : start_col + panel_tiles]
        panel_rows = chosen.transpose(1, 2, 0, 3).reshape(local_rows * TILE, PANEL)
        factor = jnp.dot(panel_rows, weights.T, precision=lax.Precision.HIGHEST)
        factor = (
            factor.reshape(local_rows, TILE, PANEL) * is_below.astype(jnp.float32)[:, None, None]
        )
        panel_piece = lax.dynamic_slice_in_dim(factor, offset * TILE, TILE, 2)
        replace = is_below[:, None, None] & holds_panel
        front_tiles = front_tiles.at[:, column_slot].set(
            jnp.where(replace, panel_piece, column_block)
        )
        received = [
            broadcast(factor, ("sib", "row"), root_step * columns + my_col)
            for root_step in range(root_count)
        ]
        column_factor = jnp.stack(received, 1).reshape(local_cols, TILE, PANEL)
        front_tiles = front_tiles - jnp.einsum(
            "aip,bjp->abij", factor, column_factor, precision=lax.Precision.HIGHEST
        )
    return front_tiles.reshape(local_rows, 1, local_cols, 1, TILE, TILE)


def route(child_rows, child_slots, tile_count, grid_rows, columns, local_cols):
    slot_ids = child_slots[0, 0]
    row_list = child_rows[0]
    slot_total = slot_ids.shape[0]
    positions = jnp.arange(CHILD_TILES, dtype=jnp.int32)

    def look_up(index):
        return jnp.sum(jnp.where(index[:, None] == positions[None, :], row_list[None, :], 0), axis=1)

    parent_row = look_up(slot_ids // CHILD_TILES)
    parent_col = look_up(slot_ids % CHILD_TILES)
    owner_index = parent_row % grid_rows * columns + parent_col % columns
    target = parent_row // grid_rows * local_cols + parent_col // columns
    slot_order = jnp.arange(slot_total, dtype=jnp.int32)
    is_live = slot_order < tile_count[0, 0]
    earlier = (
        (owner_index[:, None] == owner_index[None, :])
        & is_live[None, :]
        & (slot_order[None, :] < slot_order[:, None])
    )
    slot_rank = jnp.sum(earlier.astype(jnp.int32), axis=1)
    slot_place = jnp.where(is_live, owner_index * CAP + slot_rank, grid_rows * columns * CAP)
    return slot_place, target


def collect_kernel(local_cols, land_ref, tiles_ref, out_ref):
    out_ref[...] = jnp.zeros_like(out_ref)

    def step(n, carry):
        place = land_ref[n] - 1
        b = lax.rem(place, local_cols)

        @pl.when((place >= 0) & (b < NPANEL))
        def _():
            a = place // local_cols
            out_ref[b, a] = out_ref[b, a] + tiles_ref[n]

        return carry

    lax.fori_loop(0, land_ref.shape[0], step, 0)


def exchange_kernel(
    p_ref, s_ref, z_ref,
    g_recv, up_send, down_send,
    h_recv, x_send, y_send, core_send,
    z_send, z_recv,
):
    x = lax.axis_index("sib")
    r = lax.axis_index("row")
    z = lax.axis_index("col")
    last = lax.axis_size("col") - 1
    y, core = r // 2, lax.rem(r, 2)
    right_core = core == lax.rem(z, 2)
    is_source = right_core & (y == z // 2)
    is_relay = right_core & (y != z // 2)
    up, down = (x, r, z + 1), (x, r, z - 1)
    x_peer = (1 - x, r, z)
    y_peer = (x, lax.rem(r + 2, 4), z)
    core_peer = (x, r + 1 - 2 * core, z)
    has_up, has_down = z < last, z > 0

    def remote(src, dst, send, recv, device):
        return pltpu.make_async_remote_copy(
            src_ref=src, dst_ref=dst, send_sem=send, recv_sem=recv,
            device_id=device, device_id_type=pl.DeviceIdType.MESH,
        )

    barrier = pltpu.get_barrier_semaphore()
    for peer in (x_peer, y_peer, core_peer):
        pl.semaphore_signal(barrier, inc=1, device_id=peer, device_id_type=pl.DeviceIdType.MESH)

    @pl.when(has_up)
    def _():
        pl.semaphore_signal(barrier, inc=1, device_id=up, device_id_type=pl.DeviceIdType.MESH)

    @pl.when(has_down)
    def _():
        pl.semaphore_signal(barrier, inc=1, device_id=down, device_id_type=pl.DeviceIdType.MESH)

    pl.semaphore_wait(barrier, 3 + jnp.where(has_up, 1, 0) + jnp.where(has_down, 1, 0))

    def up_copy(src, c, p):
        return remote(src, s_ref.at[0, c, p], up_send.at[c, p], g_recv.at[c, p], up)

    def down_copy(src, c, p):
        return remote(src, s_ref.at[0, c, p], down_send.at[c, p], g_recv.at[c, p], down)

    def plane_copies(src, c, p):
        there = s_ref.at[1 + x, c, p]
        recv = h_recv.at[x, c, p]
        return (
            remote(src, there, x_send.at[c, p], recv, x_peer),
            remote(src, there, y_send.at[c, p], recv, y_peer),
            remote(src, there, core_send.at[x, c, p], recv, core_peer),
        )

    def relay_x(c, p):
        here = s_ref.at[1 + x, c, p]
        return remote(here, here, x_send.at[c, p], h_recv.at[x, c, p], x_peer)

    def to_core(k, c, p):
        here = s_ref.at[1 + k, c, p]
        return remote(here, here, core_send.at[k, c, p], h_recv.at[k, c, p], core_peer)

    def units(t):
        if t == 0:
            return [(z, None, 0)]
        return [(z - t, z >= t, -1), (z + t, z + t <= last, 1)]

    def guarded(condition, body):
        if condition is None:
            body()
        else:
            pl.when(condition)(body)

    def gather_step(p, t):
        for c, exists, side in units(t):
            def body(c=c, side=side):
                if side == 0:
                    src = p_ref.at[p]
                else:
                    src = s_ref.at[0, c, p]
                    up_copy(src, c, p).wait_recv()
                if side <= 0:
                    pl.when(has_up)(lambda: up_copy(src, c, p).start())
                if side >= 0:
                    pl.when(has_down)(lambda: down_copy(src, c, p).start())

                @pl.when(is_source)
                def _():
                    for copy in plane_copies(src, c, p):
                        copy.start()

                if side == 0:
                    s_ref[0, z, p] = p_ref[p]

            guarded(exists, body)

    def relay_step(p, t):
        for c, exists, side in units(t):
            def body(c=c):
                @pl.when(is_relay)
                def _():
                    to_core(x, c, p).wait_recv()
                    relay_x(c, p).start()
                    to_core(x, c, p).start()

                @pl.when(right_core)
                def _():
                    to_core(1 - x, c, p).wait_recv()
                    to_core(1 - x, c, p).start()

            guarded(exists, body)

    def corner_x():
        return remote(s_ref.at[0, :, 0, 0], z_ref.at[r], z_send.at[0], z_recv.at[0], x_peer)

    def corner_core():
        return remote(z_ref.at[r], z_ref.at[r], z_send.at[1], z_recv.at[1], core_peer)

    def corner_y():
        pair = z_ref.at[pl.ds(2 * y, 2)]
        return remote(pair, pair, z_send.at[2], z_recv.at[2], y_peer)

    steps = [(p, t) for p in range(NPANEL) for t in range(4)]
    for n, (p, t) in enumerate(steps):
        gather_step(p, t)
        if n:
            relay_step(*steps[n - 1])
        if n == 4:
            @pl.when(x == 1)
            def _():
                corner_x().start()
                z_ref[r] = s_ref[0, :, 0, 0]
        if n == 5:
            @pl.when(x == 0)
            def _():
                corner_x().wait_recv()

            corner_core().start()
        if n == 6:
            corner_core().wait_recv()
            corner_y().start()
    relay_step(*steps[-1])

    corner_y().wait_recv()
    pl.when(x == 1)(lambda: corner_x().wait_send())
    corner_core().wait_send()
    corner_y().wait_send()
    for p, t in steps:
        for c, exists, side in units(t):
            def body(c=c, side=side, p=p):
                src = p_ref.at[p] if side == 0 else s_ref.at[0, c, p]
                if side <= 0:
                    pl.when(has_up)(lambda: up_copy(src, c, p).wait_send())
                if side >= 0:
                    pl.when(has_down)(lambda: down_copy(src, c, p).wait_send())

                @pl.when(is_source)
                def _():
                    for copy in plane_copies(src, c, p):
                        copy.wait_send()

                @pl.when(is_relay)
                def _():
                    relay_x(c, p).wait_send()
                    to_core(x, c, p).wait_send()

                @pl.when(right_core)
                def _():
                    to_core(1 - x, c, p).wait_send()

                @pl.when(jnp.logical_not(right_core))
                def _():
                    to_core(x, c, p).wait_recv()
                    to_core(1 - x, c, p).wait_recv()

            guarded(exists, body)


def split(value):
    high = value.astype(jnp.bfloat16)
    return high, (value - high.astype(jnp.float32)).astype(jnp.bfloat16)


def dot3(left, right):
    dims = (((1,), (1,)), ((), ()))
    dot = functools.partial(lax.dot_general, dimension_numbers=dims, preferred_element_type=jnp.float32)
    return dot(left[0], right[0]) + (dot(left[0], right[1]) + dot(left[1], right[0]))


def front_kernel(
    local_cols, where_ref, land_ref, r_ref, c0_ref, c1_ref, z_ref, w_ref, tiles_ref, out_ref,
    wh, wl, qh, ql, pend, lh, ll, prod, count, place, head, link,
):
    step = pl.program_id(0)
    local_rows = out_ref.shape[0]
    b_block = out_ref.shape[1]
    group = 4

    @pl.when(step == 0)
    def _():
        for p in range(NPANEL):
            wh[p], wl[p] = split(w_ref[p])
        corner = jnp.concatenate([z_ref[:, c].reshape(PANEL, TILE) for c in range(4)], axis=1)
        qh[...], ql[...] = split(dot3(split(corner), (wh[0], wl[0])))
        for n in range(5):
            count[n] = 0

        def clear(b, carry):
            head[b] = -1
            return carry

        lax.fori_loop(0, local_cols, clear, 0)

        def chain(n, carry):
            spot = land_ref[n] - 1

            @pl.when(spot >= 0)
            def _():
                b = lax.rem(spot, local_cols)
                link[n] = head[b]
                head[b] = n

            return carry

        lax.fori_loop(0, land_ref.shape[0], chain, 0)

    def solve(kind, done):
        base = jnp.where(kind == 0, 0, group + group * lax.rem(done, 2))
        chunk = kind * (local_rows // group) + done
        block = pend[pl.ds(base, group)].reshape(group * TILE, NPANEL * PANEL)
        first = dot3(split(block[:, :PANEL]), (wh[0], wl[0]))
        first_parts = split(first)
        rest = block[:, PANEL:] - dot3(first_parts, (qh[...], ql[...]))
        second = dot3(split(rest), (wh[1], wl[1]))
        kept = []
        for m in range(group):
            spot = place[kind, done * group + m]
            tile_row = jnp.where(kind == 0, spot * 8 + where_ref[0], spot * 4 + where_ref[1])
            kept.append(jnp.where(tile_row >= 8, second[m * TILE : (m + 1) * TILE], 0.0))
        second_parts = split(jnp.concatenate(kept, axis=0))
        lh[chunk, :, :PANEL], ll[chunk, :, :PANEL] = first_parts
        lh[chunk, :, PANEL:], ll[chunk, :, PANEL:] = second_parts

    @pl.when(step < local_rows)
    def _():
        for kind, ref, slab in ((0, r_ref, 0), (1, c0_ref, 1), (1, c1_ref, 2)):
            largest = jnp.max(jnp.abs(ref[...].reshape(-1, TILE)))

            @pl.when((largest > 0) & (step * 8 + where_ref[slab] >= 4))
            def _():
                n = count[kind]
                slot = lax.rem(n, group) if kind == 0 else group + lax.rem(n, 2 * group)
                for p in range(NPANEL):
                    for c in range(4):
                        start = p * PANEL + c * TILE
                        pend[slot, :, start : start + TILE] = ref[0, c, p, 0]
                place[kind, n] = step if kind == 0 else 2 * step + slab - 1
                count[kind] = n + 1

        def flush(q, carry):
            kind, partial = q // 2, lax.rem(q, 2)
            n, done = count[kind], count[2 + kind]
            full = n >= group * done + group
            left_over = (step == local_rows - 1) & (n > group * done)

            @pl.when(((partial == 0) & full) | ((partial == 1) & left_over))
            def _():
                solve(kind, done)
                count[2 + kind] = done + 1

            return carry

        lax.fori_loop(0, 4, flush, 0)

    @pl.when(step >= local_rows)
    def _():
        b0 = (step - local_rows) * b_block
        live_rows = count[0]
        out_ref[...] = jnp.zeros_like(out_ref)
        for k in range(b_block):
            n = count[4]

            @pl.when((n < count[1]) & (place[1, n] == b0 + k))
            def _():
                @pl.when(lax.rem(n, group) == 0)
                def _():
                    column = local_rows // group + n // group

                    def multiply(i, carry):
                        prod[i] = -dot3((lh[i], ll[i]), (lh[column], ll[column]))
                        return carry

                    lax.fori_loop(0, count[2], multiply, 0)

                lane = pl.multiple_of(lax.rem(n, group) * TILE, TILE)

                def put(i, carry):
                    row = pl.multiple_of(lax.rem(i, group) * TILE, TILE)
                    out_ref[place[0, i], k] = prod[i // group, pl.ds(row, TILE), pl.ds(lane, TILE)]
                    return carry

                lax.fori_loop(0, live_rows, put, 0)
                count[4] = n + 1

            def add(n):
                a = (land_ref[n] - 1) // local_cols
                out_ref[a, k] = out_ref[a, k] + tiles_ref[n]
                return link[n]

            lax.while_loop(lambda n: n >= 0, add, head[b0 + k])

        @pl.when(b0 == 0)
        def _():
            def replace(i, carry):
                a = place[0, i]
                row = pl.multiple_of(lax.rem(i, group) * TILE, TILE)
                for p in range(NPANEL):
                    @pl.when(a * 8 + where_ref[0] >= (p + 1) * 4)
                    def _():
                        lane = pl.multiple_of(p * PANEL + where_ref[1] * TILE, TILE)
                        at = (i // group, pl.ds(row, TILE), pl.ds(lane, TILE))
                        out_ref[a, p] = lh[at].astype(jnp.float32) + ll[at].astype(jnp.float32)

                return carry

            lax.fori_loop(0, live_rows, replace, 0)


def local_fast(child_tiles, child_rows, child_slots, tile_count, inverses):
    grid_rows = lax.axis_size("sib") * lax.axis_size("row")
    columns = lax.axis_size("col")
    devices = grid_rows * columns
    tile_order = NF // TILE
    local_rows = tile_order // grid_rows
    local_cols = tile_order // columns
    axes = ("sib", "row", "col")
    slot_place, target = route(child_rows, child_slots, tile_count, grid_rows, columns, local_cols)
    outgoing = (
        jnp.zeros((devices * CAP, TILE, TILE), jnp.float32)
        .at[slot_place]
        .set(child_tiles[0, 0], mode="drop")
    )
    destined = jnp.zeros((devices * CAP,), jnp.int32).at[slot_place].set(target + 1, mode="drop")
    arrived = lax.all_to_all(
        outgoing.reshape(devices, CAP, TILE, TILE), axes, split_axis=0, concat_axis=0, tiled=True
    ).reshape(devices * CAP, TILE, TILE)
    landing = lax.all_to_all(
        destined.reshape(devices, CAP), axes, split_axis=0, concat_axis=0, tiled=True
    ).reshape(devices * CAP)

    vmem = pl.BlockSpec(memory_space=pltpu.VMEM)
    smem = pl.BlockSpec(memory_space=pltpu.SMEM)
    panels = pl.pallas_call(
        functools.partial(collect_kernel, local_cols),
        out_shape=jax.ShapeDtypeStruct((NPANEL, local_rows, TILE, TILE), jnp.float32),
        in_specs=[smem, vmem],
        out_specs=vmem,
        compiler_params=pltpu.CompilerParams(vmem_limit_bytes=24 * 2**20),
        name="collect",
    )(landing, arrived)

    dma = pltpu.SemaphoreType.DMA
    unit = (columns, NPANEL)
    slabs, corner = pl.pallas_call(
        exchange_kernel,
        out_shape=(
            jax.ShapeDtypeStruct((3, columns, NPANEL, local_rows, TILE, TILE), jnp.float32),
            jax.ShapeDtypeStruct((4, columns, TILE, TILE), jnp.float32),
        ),
        in_specs=[vmem],
        out_specs=(vmem, vmem),
        scratch_shapes=[
            dma(unit), dma(unit), dma(unit),
            dma((2,) + unit), dma(unit), dma(unit), dma((2,) + unit),
            dma((3,)), dma((3,)),
        ],
        compiler_params=pltpu.CompilerParams(
            collective_id=0, has_side_effects=True, vmem_limit_bytes=40 * 2**20
        ),
        name="exchange",
    )(panels)

    my_row = lax.axis_index(("sib", "row"))
    my_col = lax.axis_index("col")
    my_sib = lax.axis_index("sib")
    is_source = lax.axis_index("row") == my_col
    picks = [jnp.where(is_source & (my_sib == k), 0, 1 + k) for k in range(2)]
    where = jnp.stack([my_row, my_col, my_col + 4, my_col, 0 * my_col, *picks]).astype(jnp.int32)
    b_block = 2
    order = NPANEL * PANEL
    group = 4
    scalar = pltpu.SMEM
    last = local_rows - 1

    def slab_spec(slab):
        return pl.BlockSpec(
            (1, columns, NPANEL, 1, TILE, TILE),
            lambda j, w, l: (w[4 + slab], 0, 0, jnp.minimum(j, last), 0, 0),
        )

    def whole(*shape):
        return pl.BlockSpec(shape, lambda j, w, l: (0,) * len(shape), pipeline_mode=pl.Buffered(1))

    front = pl.pallas_call(
        functools.partial(front_kernel, local_cols),
        grid_spec=pltpu.PrefetchScalarGridSpec(
            num_scalar_prefetch=2,
            grid=(local_rows + local_cols // b_block,),
            in_specs=[
                slab_spec(0), slab_spec(1), slab_spec(2),
                whole(4, columns, TILE, TILE),
                whole(NPANEL, PANEL, PANEL),
                whole(devices * CAP, TILE, TILE),
            ],
            out_specs=pl.BlockSpec(
                (local_rows, b_block, TILE, TILE),
                lambda j, w, l: (0, jnp.maximum(j - local_rows, 0), 0, 0),
            ),
            scratch_shapes=[
                pltpu.VMEM((NPANEL, PANEL, PANEL), jnp.bfloat16),
                pltpu.VMEM((NPANEL, PANEL, PANEL), jnp.bfloat16),
                pltpu.VMEM((PANEL, PANEL), jnp.bfloat16),
                pltpu.VMEM((PANEL, PANEL), jnp.bfloat16),
                pltpu.VMEM((3 * group, TILE, order), jnp.float32),
                pltpu.VMEM(((local_rows + local_cols) // group, group * TILE, order), jnp.bfloat16),
                pltpu.VMEM(((local_rows + local_cols) // group, group * TILE, order), jnp.bfloat16),
                pltpu.VMEM((local_rows // group, group * TILE, group * TILE), jnp.float32),
                scalar((8,), jnp.int32),
                scalar((2, local_cols + group), jnp.int32),
                scalar((local_cols,), jnp.int32),
                scalar((devices * CAP,), jnp.int32),
            ],
        ),
        out_shape=jax.ShapeDtypeStruct((local_rows, local_cols, TILE, TILE), jnp.float32),
        compiler_params=pltpu.CompilerParams(vmem_limit_bytes=62 * 2**20),
        name="front",
    )(where, landing, slabs, slabs, slabs, corner, inverses, arrived)
    return front.reshape(local_rows, 1, local_cols, 1, TILE, TILE)


def solution(mesh):
    sizes = (mesh.shape["sib"], mesh.shape["row"], mesh.shape["col"])
    return jax.shard_map(
        local_fast if sizes == (2, 4, 4) else local,
        mesh=mesh,
        in_specs=(
            P("sib", ("row", "col"), None, None, None),
            P("sib", None),
            P("sib", ("row", "col"), None),
            P("sib", ("row", "col")),
            P(),
        ),
        out_specs=P(None, ("sib", "row"), None, "col", None, None),
        check_vma=False,
    )
```

```python
import functools

import jax
import jax.numpy as jnp
from jax import lax
from jax.experimental import pallas as pl
from jax.experimental.pallas import tpu as pltpu
from jax.sharding import PartitionSpec as P

NF = 16384
TILE = 128
PANEL = 512
NPANEL = 2
CHILD_TILES = 64
CAP = 2
PACK = 11


def broadcast(value, axis, source):
    kept = jnp.where(lax.axis_index(axis) == source, value, 0).astype(value.dtype)
    return lax.psum(kept, axis)


def local(child_tiles, child_rows, child_slots, tile_count, inverses):
    grid_rows = lax.axis_size("sib") * lax.axis_size("row")
    columns = lax.axis_size("col")
    devices = grid_rows * columns
    tile_order = NF // TILE
    local_rows = tile_order // grid_rows
    local_cols = tile_order // columns
    tile_data = child_tiles[0, 0]
    slot_ids = child_slots[0, 0]
    live_count = tile_count[0, 0]
    row_list = child_rows[0]
    slot_total = slot_ids.shape[0]
    child_row = slot_ids // CHILD_TILES
    child_col = slot_ids % CHILD_TILES
    positions = jnp.arange(CHILD_TILES, dtype=jnp.int32)
    parent_row = jnp.sum(
        jnp.where(child_row[:, None] == positions[None, :], row_list[None, :], 0), axis=1
    )
    parent_col = jnp.sum(
        jnp.where(child_col[:, None] == positions[None, :], row_list[None, :], 0), axis=1
    )
    owner_index = parent_row % grid_rows * columns + parent_col % columns
    target = parent_row // grid_rows * local_cols + parent_col // columns
    slot_order = jnp.arange(slot_total, dtype=jnp.int32)
    is_live = slot_order < live_count
    earlier = (
        (owner_index[:, None] == owner_index[None, :])
        & is_live[None, :]
        & (slot_order[None, :] < slot_order[:, None])
    )
    slot_rank = jnp.sum(earlier.astype(jnp.int32), axis=1)
    slot_place = jnp.where(is_live, owner_index * CAP + slot_rank, devices * CAP)
    outgoing = (
        jnp.zeros((devices * CAP, TILE, TILE), jnp.float32)
        .at[slot_place]
        .set(tile_data, mode="drop")
    )
    destined = jnp.zeros((devices * CAP,), jnp.int32).at[slot_place].set(target, mode="drop")
    arrived, landing = (
        lax.all_to_all(
            outgoing.reshape(devices, CAP, TILE, TILE),
            ("sib", "row", "col"),
            split_axis=0,
            concat_axis=0,
            tiled=True,
        ),
        lax.all_to_all(
            destined.reshape(devices, CAP),
            ("sib", "row", "col"),
            split_axis=0,
            concat_axis=0,
            tiled=True,
        ),
    )
    front_tiles = jnp.zeros((local_rows * local_cols, TILE, TILE), jnp.float32)
    front_tiles = front_tiles.at[landing.reshape(-1)].add(arrived.reshape(-1, TILE, TILE))
    front_tiles = front_tiles.reshape(local_rows, local_cols, TILE, TILE)
    my_row = lax.axis_index(("sib", "row"))
    my_col = lax.axis_index("col")
    panel_tiles = PANEL // TILE
    root_count = grid_rows // columns
    tile_ids = jnp.arange(local_rows, dtype=jnp.int32) * grid_rows + my_row
    for panel_step in range(NPANEL):
        first_tile = panel_tiles * panel_step
        below_tile = first_tile + panel_tiles
        column_slot = first_tile // columns
        start_col = first_tile % columns
        is_below = tile_ids >= below_tile
        weights = inverses[panel_step]
        column_block = front_tiles[:, column_slot]
        holds_panel = (my_col >= start_col) & (my_col < start_col + panel_tiles)
        offset = jnp.clip(my_col - start_col, 0, panel_tiles - 1)
        everyone = lax.all_gather(column_block[None], "col", axis=0, tiled=True)
        chosen = everyone[start_col : start_col + panel_tiles]
        panel_rows = chosen.transpose(1, 2, 0, 3).reshape(local_rows * TILE, PANEL)
        factor = jnp.dot(panel_rows, weights.T, precision=lax.Precision.HIGHEST)
        factor = (
            factor.reshape(local_rows, TILE, PANEL) * is_below.astype(jnp.float32)[:, None, None]
        )
        panel_piece = lax.dynamic_slice_in_dim(factor, offset * TILE, TILE, 2)
        replace = is_below[:, None, None] & holds_panel
        front_tiles = front_tiles.at[:, column_slot].set(
            jnp.where(replace, panel_piece, column_block)
        )
        received = [
            broadcast(factor, ("sib", "row"), root_step * columns + my_col)
            for root_step in range(root_count)
        ]
        column_factor = jnp.stack(received, 1).reshape(local_cols, TILE, PANEL)
        front_tiles = front_tiles - jnp.einsum(
            "aip,bjp->abij", factor, column_factor, precision=lax.Precision.HIGHEST
        )
    return front_tiles.reshape(local_rows, 1, local_cols, 1, TILE, TILE)


def route(child_rows, child_slots, tile_count, grid_rows, columns, local_cols):
    slot_ids = child_slots[0, 0]
    row_list = child_rows[0]
    slot_total = slot_ids.shape[0]
    positions = jnp.arange(CHILD_TILES, dtype=jnp.int32)

    def look_up(index):
        return jnp.sum(jnp.where(index[:, None] == positions[None, :], row_list[None, :], 0), axis=1)

    parent_row = look_up(slot_ids // CHILD_TILES)
    parent_col = look_up(slot_ids % CHILD_TILES)
    owner_index = parent_row % grid_rows * columns + parent_col % columns
    target = parent_row // grid_rows * local_cols + parent_col // columns
    slot_order = jnp.arange(slot_total, dtype=jnp.int32)
    is_live = slot_order < tile_count[0, 0]
    earlier = (
        (owner_index[:, None] == owner_index[None, :])
        & is_live[None, :]
        & (slot_order[None, :] < slot_order[:, None])
    )
    slot_rank = jnp.sum(earlier.astype(jnp.int32), axis=1)
    slot_place = jnp.where(is_live, owner_index * CAP + slot_rank, grid_rows * columns * CAP)
    return slot_place, target


def collect_kernel(local_cols, land_ref, table_ref, tiles_ref, out_ref, pack_ref):
    out_ref[...] = jnp.zeros_like(out_ref)

    def step(n, carry):
        place = land_ref[n] - 1
        b = lax.rem(place, local_cols)

        @pl.when((place >= 0) & (b < NPANEL))
        def _():
            a = place // local_cols
            out_ref[b, a] = out_ref[b, a] + tiles_ref[n]

        return carry

    lax.fori_loop(0, land_ref.shape[0], step, 0)
    pack_ref[...] = jnp.zeros_like(pack_ref)

    def pack(n, carry):
        slot = table_ref[n]

        @pl.when((slot >= 0) & (slot < PACK))
        def _():
            pack_ref[0, slot] = out_ref[lax.rem(n, NPANEL), n // NPANEL]

        return carry

    lax.fori_loop(0, table_ref.shape[0], pack, 0)


def exchange_kernel(
    p_ref, s_ref, z_ref,
    g_recv, up_send, down_send,
    h_recv, x_send, y_send, core_send,
    z_send, z_recv,
):
    x = lax.axis_index("sib")
    r = lax.axis_index("row")
    z = lax.axis_index("col")
    last = lax.axis_size("col") - 1
    y, core = r // 2, lax.rem(r, 2)
    right_core = core == lax.rem(z, 2)
    is_source = right_core & (y == z // 2)
    is_relay = right_core & (y != z // 2)
    up, down = (x, r, z + 1), (x, r, z - 1)
    x_peer = (1 - x, r, z)
    y_peer = (x, lax.rem(r + 2, 4), z)
    core_peer = (x, r + 1 - 2 * core, z)
    has_up, has_down = z < last, z > 0

    def remote(src, dst, send, recv, device):
        return pltpu.make_async_remote_copy(
            src_ref=src, dst_ref=dst, send_sem=send, recv_sem=recv,
            device_id=device, device_id_type=pl.DeviceIdType.MESH,
        )

    barrier = pltpu.get_barrier_semaphore()
    for peer in (x_peer, y_peer, core_peer):
        pl.semaphore_signal(barrier, inc=1, device_id=peer, device_id_type=pl.DeviceIdType.MESH)

    @pl.when(has_up)
    def _():
        pl.semaphore_signal(barrier, inc=1, device_id=up, device_id_type=pl.DeviceIdType.MESH)

    @pl.when(has_down)
    def _():
        pl.semaphore_signal(barrier, inc=1, device_id=down, device_id_type=pl.DeviceIdType.MESH)

    pl.semaphore_wait(barrier, 3 + jnp.where(has_up, 1, 0) + jnp.where(has_down, 1, 0))

    def up_copy(src, c, p):
        return remote(src, s_ref.at[0, c, p], up_send.at[c, p], g_recv.at[c, p], up)

    def down_copy(src, c, p):
        return remote(src, s_ref.at[0, c, p], down_send.at[c, p], g_recv.at[c, p], down)

    def plane_copies(src, c, p):
        there = s_ref.at[1 + x, c, p]
        recv = h_recv.at[x, c, p]
        return (
            remote(src, there, x_send.at[c, p], recv, x_peer),
            remote(src, there, y_send.at[c, p], recv, y_peer),
            remote(src, there, core_send.at[x, c, p], recv, core_peer),
        )

    def relay_x(c, p):
        here = s_ref.at[1 + x, c, p]
        return remote(here, here, x_send.at[c, p], h_recv.at[x, c, p], x_peer)

    def to_core(k, c, p):
        here = s_ref.at[1 + k, c, p]
        return remote(here, here, core_send.at[k, c, p], h_recv.at[k, c, p], core_peer)

    def units(t):
        if t == 0:
            return [(z, None, 0)]
        return [(z - t, z >= t, -1), (z + t, z + t <= last, 1)]

    def guarded(condition, body):
        if condition is None:
            body()
        else:
            pl.when(condition)(body)

    def gather_step(p, t):
        for c, exists, side in units(t):
            def body(c=c, side=side):
                if side == 0:
                    src = p_ref.at[p]
                else:
                    src = s_ref.at[0, c, p]
                    up_copy(src, c, p).wait_recv()
                if side <= 0:
                    pl.when(has_up)(lambda: up_copy(src, c, p).start())
                if side >= 0:
                    pl.when(has_down)(lambda: down_copy(src, c, p).start())

                @pl.when(is_source)
                def _():
                    for copy in plane_copies(src, c, p):
                        copy.start()

                if side == 0:
                    s_ref[0, z, p] = p_ref[p]

            guarded(exists, body)

    def relay_step(p, t):
        for c, exists, side in units(t):
            def body(c=c):
                @pl.when(is_relay)
                def _():
                    to_core(x, c, p).wait_recv()
                    relay_x(c, p).start()
                    to_core(x, c, p).start()

                @pl.when(right_core)
                def _():
                    to_core(1 - x, c, p).wait_recv()
                    to_core(1 - x, c, p).start()

            guarded(exists, body)

    def corner_x():
        return remote(s_ref.at[0, :, 0, 0], z_ref.at[r], z_send.at[0], z_recv.at[0], x_peer)

    def corner_core():
        return remote(z_ref.at[r], z_ref.at[r], z_send.at[1], z_recv.at[1], core_peer)

    def corner_y():
        pair = z_ref.at[pl.ds(2 * y, 2)]
        return remote(pair, pair, z_send.at[2], z_recv.at[2], y_peer)

    def corner_first():
        @pl.when(x == 1)
        def _():
            corner_x().start()
            z_ref[r] = s_ref[0, :, 0, 0]

    def corner_second():
        @pl.when(x == 0)
        def _():
            corner_x().wait_recv()

        corner_core().start()

    def corner_third():
        corner_core().wait_recv()
        corner_y().start()

    corner_steps = [corner_first, corner_second, corner_third]
    steps = [(p, t) for p in range(p_ref.shape[0]) for t in range(4)]
    for n, (p, t) in enumerate(steps):
        gather_step(p, t)
        if n >= 3 and corner_steps:
            corner_steps.pop(0)()
        if n:
            relay_step(*steps[n - 1])
    relay_step(*steps[-1])
    for corner_step in corner_steps:
        corner_step()

    corner_y().wait_recv()
    pl.when(x == 1)(lambda: corner_x().wait_send())
    corner_core().wait_send()
    corner_y().wait_send()
    for p, t in steps:
        for c, exists, side in units(t):
            def body(c=c, side=side, p=p):
                src = p_ref.at[p] if side == 0 else s_ref.at[0, c, p]
                if side <= 0:
                    pl.when(has_up)(lambda: up_copy(src, c, p).wait_send())
                if side >= 0:
                    pl.when(has_down)(lambda: down_copy(src, c, p).wait_send())

                @pl.when(is_source)
                def _():
                    for copy in plane_copies(src, c, p):
                        copy.wait_send()

                @pl.when(is_relay)
                def _():
                    relay_x(c, p).wait_send()
                    to_core(x, c, p).wait_send()

                @pl.when(right_core)
                def _():
                    to_core(1 - x, c, p).wait_send()

                @pl.when(jnp.logical_not(right_core))
                def _():
                    to_core(x, c, p).wait_recv()
                    to_core(1 - x, c, p).wait_recv()

            guarded(exists, body)


def split(value):
    high = value.astype(jnp.bfloat16)
    return high, (value - high.astype(jnp.float32)).astype(jnp.bfloat16)


def dot3(left, right):
    dims = (((1,), (1,)), ((), ()))
    dot = functools.partial(lax.dot_general, dimension_numbers=dims, preferred_element_type=jnp.float32)
    return dot(left[0], right[0]) + (dot(left[0], right[1]) + dot(left[1], right[0]))


def front_kernel(local_cols, packed, where_ref, land_ref, *refs):
    if packed:
        table_ref, packs_ref, *refs = refs
    else:
        r_ref, c0_ref, c1_ref, *refs = refs
    z_ref, w_ref, tiles_ref, out_ref, wh, wl, qh, ql, pend, lh, ll, prod, count, place, head, link = refs
    step = pl.program_id(0)
    local_rows = out_ref.shape[0]
    b_block = out_ref.shape[1]
    group = 4
    solve_steps = 1 if packed else local_rows

    @pl.when(step == 0)
    def _():
        for p in range(NPANEL):
            wh[p], wl[p] = split(w_ref[p])
        corner = jnp.concatenate([z_ref[:, c].reshape(PANEL, TILE) for c in range(4)], axis=1)
        qh[...], ql[...] = split(dot3(split(corner), (wh[0], wl[0])))
        for n in range(5):
            count[n] = 0

        def clear(b, carry):
            head[b] = -1
            return carry

        lax.fori_loop(0, local_cols, clear, 0)

        def chain(n, carry):
            spot = land_ref[n] - 1

            @pl.when(spot >= 0)
            def _():
                b = lax.rem(spot, local_cols)
                link[n] = head[b]
                head[b] = n

            return carry

        lax.fori_loop(0, land_ref.shape[0], chain, 0)

    def solve(kind, done):
        base = jnp.where(kind == 0, 0, group + group * lax.rem(done, 2))
        chunk = kind * (local_rows // group) + done
        block = pend[pl.ds(base, group)].reshape(group * TILE, NPANEL * PANEL)
        first = dot3(split(block[:, :PANEL]), (wh[0], wl[0]))
        first_parts = split(first)
        rest = block[:, PANEL:] - dot3(first_parts, (qh[...], ql[...]))
        second = dot3(split(rest), (wh[1], wl[1]))
        kept = []
        for m in range(group):
            spot = place[kind, done * group + m]
            tile_row = jnp.where(kind == 0, spot * 8 + where_ref[0], spot * 4 + where_ref[1])
            kept.append(jnp.where(tile_row >= 8, second[m * TILE : (m + 1) * TILE], 0.0))
        second_parts = split(jnp.concatenate(kept, axis=0))
        lh[chunk, :, :PANEL], ll[chunk, :, :PANEL] = first_parts
        lh[chunk, :, PANEL:], ll[chunk, :, PANEL:] = second_parts

    def take(a):
        for kind, slab in ((0, 0), (1, 1), (1, 2)):
            if packed:
                spots = [
                    [table_ref[((slab * 4 + c) * local_rows + a) * NPANEL + p] for c in range(4)]
                    for p in range(NPANEL)
                ]
                largest = functools.reduce(jnp.maximum, spots[0] + spots[1])
                is_live = largest >= 0
            else:
                ref = (r_ref, c0_ref, c1_ref)[slab]
                is_live = jnp.max(jnp.abs(ref[...].reshape(-1, TILE))) > 0

            @pl.when(is_live & (a * 8 + where_ref[slab] >= 4))
            def _():
                n = count[kind]
                slot = lax.rem(n, group) if kind == 0 else group + lax.rem(n, 2 * group)
                for p in range(NPANEL):
                    for c in range(4):
                        start = p * PANEL + c * TILE
                        if packed:
                            spot = spots[p][c]
                            tile = packs_ref[where_ref[4 + slab], c, 0, jnp.maximum(spot, 0)]
                            tile = jnp.where(spot >= 0, tile, 0.0)
                        else:
                            tile = ref[0, c, p, 0]
                        pend[slot, :, start : start + TILE] = tile
                place[kind, n] = a if kind == 0 else 2 * a + slab - 1
                count[kind] = n + 1

        def flush(q, carry):
            kind, partial = q // 2, lax.rem(q, 2)
            n, done = count[kind], count[2 + kind]
            full = n >= group * done + group
            left_over = (a == local_rows - 1) & (n > group * done)

            @pl.when(((partial == 0) & full) | ((partial == 1) & left_over))
            def _():
                solve(kind, done)
                count[2 + kind] = done + 1

            return carry

        lax.fori_loop(0, 4, flush, 0)

    @pl.when(step < solve_steps)
    def _():
        if packed:
            def take_one(a, carry):
                take(a)
                return carry

            lax.fori_loop(0, local_rows, take_one, 0)
        else:
            take(step)

    @pl.when(step >= solve_steps)
    def _():
        b0 = (step - solve_steps) * b_block
        live_rows = count[0]
        out_ref[...] = jnp.zeros_like(out_ref)
        for k in range(b_block):
            n = count[4]

            @pl.when((n < count[1]) & (place[1, n] == b0 + k))
            def _():
                @pl.when(lax.rem(n, group) == 0)
                def _():
                    column = local_rows // group + n // group

                    def multiply(i, carry):
                        prod[i] = -dot3((lh[i], ll[i]), (lh[column], ll[column]))
                        return carry

                    lax.fori_loop(0, count[2], multiply, 0)

                lane = pl.multiple_of(lax.rem(n, group) * TILE, TILE)

                def put(i, carry):
                    row = pl.multiple_of(lax.rem(i, group) * TILE, TILE)
                    out_ref[place[0, i], k] = prod[i // group, pl.ds(row, TILE), pl.ds(lane, TILE)]
                    return carry

                lax.fori_loop(0, live_rows, put, 0)
                count[4] = n + 1

            def add(n):
                a = (land_ref[n] - 1) // local_cols
                out_ref[a, k] = out_ref[a, k] + tiles_ref[n]
                return link[n]

            lax.while_loop(lambda n: n >= 0, add, head[b0 + k])

        @pl.when(b0 == 0)
        def _():
            def replace(i, carry):
                a = place[0, i]
                row = pl.multiple_of(lax.rem(i, group) * TILE, TILE)
                for p in range(NPANEL):
                    @pl.when(a * 8 + where_ref[0] >= (p + 1) * 4)
                    def _():
                        lane = pl.multiple_of(p * PANEL + where_ref[1] * TILE, TILE)
                        at = (i // group, pl.ds(row, TILE), pl.ds(lane, TILE))
                        out_ref[a, p] = lh[at].astype(jnp.float32) + ll[at].astype(jnp.float32)

                return carry

            lax.fori_loop(0, live_rows, replace, 0)


def local_fast(child_tiles, child_rows, child_slots, tile_count, inverses):
    grid_rows = lax.axis_size("sib") * lax.axis_size("row")
    columns = lax.axis_size("col")
    devices = grid_rows * columns
    tile_order = NF // TILE
    local_rows = tile_order // grid_rows
    local_cols = tile_order // columns
    axes = ("sib", "row", "col")
    slot_place, target = route(child_rows, child_slots, tile_count, grid_rows, columns, local_cols)
    outgoing = (
        jnp.zeros((devices * CAP, TILE, TILE), jnp.float32)
        .at[slot_place]
        .set(child_tiles[0, 0], mode="drop")
    )
    destined = jnp.zeros((devices * CAP,), jnp.int32).at[slot_place].set(target + 1, mode="drop")
    arrived = lax.all_to_all(
        outgoing.reshape(devices, CAP, TILE, TILE), axes, split_axis=0, concat_axis=0, tiled=True
    ).reshape(devices * CAP, TILE, TILE)
    landing = lax.all_to_all(
        destined.reshape(devices, CAP), axes, split_axis=0, concat_axis=0, tiled=True
    ).reshape(devices * CAP)

    vmem = pl.BlockSpec(memory_space=pltpu.VMEM)
    smem = pl.BlockSpec(memory_space=pltpu.SMEM)
    spot = landing - 1
    panel_spot = jnp.where(
        (landing > 0) & (spot % local_cols < NPANEL),
        spot // local_cols * NPANEL + spot % local_cols,
        0,
    )
    all_places = jnp.arange(local_rows * NPANEL, dtype=jnp.int32)
    is_live = jnp.any(panel_spot[None, :] == all_places[:, None], axis=1) | (all_places == 0)
    earlier = is_live[None, :] & (all_places[None, :] < all_places[:, None])
    table = jnp.where(is_live, jnp.sum(earlier.astype(jnp.int32), axis=1), -1)
    tables = lax.all_gather(table, axes, axis=0, tiled=False)
    fits = jnp.max(tables) < PACK

    panels, pack = pl.pallas_call(
        functools.partial(collect_kernel, local_cols),
        out_shape=(
            jax.ShapeDtypeStruct((NPANEL, local_rows, TILE, TILE), jnp.float32),
            jax.ShapeDtypeStruct((1, PACK, TILE, TILE), jnp.float32),
        ),
        in_specs=[smem, smem, vmem],
        out_specs=(vmem, vmem),
        compiler_params=pltpu.CompilerParams(vmem_limit_bytes=24 * 2**20),
        name="collect",
    )(landing, table, arrived)

    my_sib = lax.axis_index("sib")
    my_row = lax.axis_index(("sib", "row"))
    my_col = lax.axis_index("col")
    is_source = lax.axis_index("row") == my_col
    picks = [jnp.where(is_source & (my_sib == k), 0, 1 + k) for k in range(2)]
    where = jnp.stack([my_row, my_col, my_col + 4, my_col, 0 * my_col, *picks]).astype(jnp.int32)
    by_grid_row = tables.reshape(grid_rows, columns * local_rows * NPANEL)
    slab_tables = jnp.concatenate(
        [lax.dynamic_index_in_dim(by_grid_row, g, 0, False) for g in (my_row, my_col, my_col + 4)]
    )

    dma = pltpu.SemaphoreType.DMA

    def exchange(block, collective_id, name):
        unit = (columns, block.shape[0])
        return pl.pallas_call(
            exchange_kernel,
            out_shape=(
                jax.ShapeDtypeStruct((3, columns, *block.shape), jnp.float32),
                jax.ShapeDtypeStruct((4, columns, TILE, TILE), jnp.float32),
            ),
            in_specs=[vmem],
            out_specs=(vmem, vmem),
            scratch_shapes=[
                dma(unit), dma(unit), dma(unit),
                dma((2,) + unit), dma(unit), dma(unit), dma((2,) + unit),
                dma((3,)), dma((3,)),
            ],
            compiler_params=pltpu.CompilerParams(
                collective_id=collective_id, has_side_effects=True, vmem_limit_bytes=40 * 2**20
            ),
            name=name,
        )(block)

    b_block = 2
    order = NPANEL * PANEL
    group = 4
    last = local_rows - 1

    def slab_spec(slab):
        return pl.BlockSpec(
            (1, columns, NPANEL, 1, TILE, TILE),
            lambda j, w, l: (w[4 + slab], 0, 0, jnp.minimum(j, last), 0, 0),
        )

    def whole(*shape):
        return pl.BlockSpec(shape, lambda j, w, l: (0,) * len(shape), pipeline_mode=pl.Buffered(1))

    def finish(packed, slab_specs, slab_args, corner, name):
        solve_steps = 1 if packed else local_rows
        return pl.pallas_call(
            functools.partial(front_kernel, local_cols, packed),
            grid_spec=pltpu.PrefetchScalarGridSpec(
                num_scalar_prefetch=2,
                grid=(solve_steps + local_cols // b_block,),
                in_specs=[
                    *slab_specs,
                    whole(4, columns, TILE, TILE),
                    whole(NPANEL, PANEL, PANEL),
                    whole(devices * CAP, TILE, TILE),
                ],
                out_specs=pl.BlockSpec(
                    (local_rows, b_block, TILE, TILE),
                    lambda j, w, l: (0, jnp.maximum(j - solve_steps, 0), 0, 0),
                ),
                scratch_shapes=[
                    pltpu.VMEM((NPANEL, PANEL, PANEL), jnp.bfloat16),
                    pltpu.VMEM((NPANEL, PANEL, PANEL), jnp.bfloat16),
                    pltpu.VMEM((PANEL, PANEL), jnp.bfloat16),
                    pltpu.VMEM((PANEL, PANEL), jnp.bfloat16),
                    pltpu.VMEM((3 * group, TILE, order), jnp.float32),
                    pltpu.VMEM(((local_rows + local_cols) // group, group * TILE, order), jnp.bfloat16),
                    pltpu.VMEM(((local_rows + local_cols) // group, group * TILE, order), jnp.bfloat16),
                    pltpu.VMEM((local_rows // group, group * TILE, group * TILE), jnp.float32),
                    pltpu.SMEM((8,), jnp.int32),
                    pltpu.SMEM((2, local_cols + group), jnp.int32),
                    pltpu.SMEM((local_cols,), jnp.int32),
                    pltpu.SMEM((devices * CAP,), jnp.int32),
                ],
            ),
            out_shape=jax.ShapeDtypeStruct((local_rows, local_cols, TILE, TILE), jnp.float32),
            compiler_params=pltpu.CompilerParams(vmem_limit_bytes=62 * 2**20),
            name=name,
        )(where, landing, *slab_args, corner, inverses, arrived)

    def by_packs():
        packs, corner = exchange(pack, 1, "exchange_packs")
        specs = [smem, whole(3, columns, 1, PACK, TILE, TILE)]
        return finish(True, specs, [slab_tables, packs], corner, "front_packs")

    def by_panels():
        slabs, corner = exchange(panels, 0, "exchange_panels")
        return finish(False, [slab_spec(k) for k in range(3)], [slabs] * 3, corner, "front_panels")

    front = lax.cond(fits, by_packs, by_panels)
    return front.reshape(local_rows, 1, local_cols, 1, TILE, TILE)


def solution(mesh):
    sizes = (mesh.shape["sib"], mesh.shape["row"], mesh.shape["col"])
    return jax.shard_map(
        local_fast if sizes == (2, 4, 4) else local,
        mesh=mesh,
        in_specs=(
            P("sib", ("row", "col"), None, None, None),
            P("sib", None),
            P("sib", ("row", "col"), None),
            P("sib", ("row", "col")),
            P(),
        ),
        out_specs=P(None, ("sib", "row"), None, "col", None, None),
        check_vma=False,
    )
```

```python
import functools

import jax
import jax.numpy as jnp
from jax import lax
from jax.experimental import pallas as pl
from jax.experimental.pallas import tpu as pltpu
from jax.sharding import PartitionSpec as P

NF = 16384
TILE = 128
PANEL = 512
NPANEL = 2
CHILD_TILES = 64
CAP = 2
PACK = 10
PACK_PARTS = 2


def broadcast(value, axis, source):
    kept = jnp.where(lax.axis_index(axis) == source, value, 0).astype(value.dtype)
    return lax.psum(kept, axis)


def local(child_tiles, child_rows, child_slots, tile_count, inverses):
    grid_rows = lax.axis_size("sib") * lax.axis_size("row")
    columns = lax.axis_size("col")
    devices = grid_rows * columns
    tile_order = NF // TILE
    local_rows = tile_order // grid_rows
    local_cols = tile_order // columns
    tile_data = child_tiles[0, 0]
    slot_ids = child_slots[0, 0]
    live_count = tile_count[0, 0]
    row_list = child_rows[0]
    slot_total = slot_ids.shape[0]
    child_row = slot_ids // CHILD_TILES
    child_col = slot_ids % CHILD_TILES
    positions = jnp.arange(CHILD_TILES, dtype=jnp.int32)
    parent_row = jnp.sum(
        jnp.where(child_row[:, None] == positions[None, :], row_list[None, :], 0), axis=1
    )
    parent_col = jnp.sum(
        jnp.where(child_col[:, None] == positions[None, :], row_list[None, :], 0), axis=1
    )
    owner_index = parent_row % grid_rows * columns + parent_col % columns
    target = parent_row // grid_rows * local_cols + parent_col // columns
    slot_order = jnp.arange(slot_total, dtype=jnp.int32)
    is_live = slot_order < live_count
    earlier = (
        (owner_index[:, None] == owner_index[None, :])
        & is_live[None, :]
        & (slot_order[None, :] < slot_order[:, None])
    )
    slot_rank = jnp.sum(earlier.astype(jnp.int32), axis=1)
    slot_place = jnp.where(is_live, owner_index * CAP + slot_rank, devices * CAP)
    outgoing = (
        jnp.zeros((devices * CAP, TILE, TILE), jnp.float32)
        .at[slot_place]
        .set(tile_data, mode="drop")
    )
    destined = jnp.zeros((devices * CAP,), jnp.int32).at[slot_place].set(target, mode="drop")
    arrived, landing = (
        lax.all_to_all(
            outgoing.reshape(devices, CAP, TILE, TILE),
            ("sib", "row", "col"),
            split_axis=0,
            concat_axis=0,
            tiled=True,
        ),
        lax.all_to_all(
            destined.reshape(devices, CAP),
            ("sib", "row", "col"),
            split_axis=0,
            concat_axis=0,
            tiled=True,
        ),
    )
    front_tiles = jnp.zeros((local_rows * local_cols, TILE, TILE), jnp.float32)
    front_tiles = front_tiles.at[landing.reshape(-1)].add(arrived.reshape(-1, TILE, TILE))
    front_tiles = front_tiles.reshape(local_rows, local_cols, TILE, TILE)
    my_row = lax.axis_index(("sib", "row"))
    my_col = lax.axis_index("col")
    panel_tiles = PANEL // TILE
    root_count = grid_rows // columns
    tile_ids = jnp.arange(local_rows, dtype=jnp.int32) * grid_rows + my_row
    for panel_step in range(NPANEL):
        first_tile = panel_tiles * panel_step
        below_tile = first_tile + panel_tiles
        column_slot = first_tile // columns
        start_col = first_tile % columns
        is_below = tile_ids >= below_tile
        weights = inverses[panel_step]
        column_block = front_tiles[:, column_slot]
        holds_panel = (my_col >= start_col) & (my_col < start_col + panel_tiles)
        offset = jnp.clip(my_col - start_col, 0, panel_tiles - 1)
        everyone = lax.all_gather(column_block[None], "col", axis=0, tiled=True)
        chosen = everyone[start_col : start_col + panel_tiles]
        panel_rows = chosen.transpose(1, 2, 0, 3).reshape(local_rows * TILE, PANEL)
        factor = jnp.dot(panel_rows, weights.T, precision=lax.Precision.HIGHEST)
        factor = (
            factor.reshape(local_rows, TILE, PANEL) * is_below.astype(jnp.float32)[:, None, None]
        )
        panel_piece = lax.dynamic_slice_in_dim(factor, offset * TILE, TILE, 2)
        replace = is_below[:, None, None] & holds_panel
        front_tiles = front_tiles.at[:, column_slot].set(
            jnp.where(replace, panel_piece, column_block)
        )
        received = [
            broadcast(factor, ("sib", "row"), root_step * columns + my_col)
            for root_step in range(root_count)
        ]
        column_factor = jnp.stack(received, 1).reshape(local_cols, TILE, PANEL)
        front_tiles = front_tiles - jnp.einsum(
            "aip,bjp->abij", factor, column_factor, precision=lax.Precision.HIGHEST
        )
    return front_tiles.reshape(local_rows, 1, local_cols, 1, TILE, TILE)


def route(child_rows, child_slots, tile_count, grid_rows, columns, local_cols):
    slot_ids = child_slots[0, 0]
    row_list = child_rows[0]
    slot_total = slot_ids.shape[0]
    positions = jnp.arange(CHILD_TILES, dtype=jnp.int32)

    def look_up(index):
        return jnp.sum(jnp.where(index[:, None] == positions[None, :], row_list[None, :], 0), axis=1)

    parent_row = look_up(slot_ids // CHILD_TILES)
    parent_col = look_up(slot_ids % CHILD_TILES)
    owner_index = parent_row % grid_rows * columns + parent_col % columns
    target = parent_row // grid_rows * local_cols + parent_col // columns
    slot_order = jnp.arange(slot_total, dtype=jnp.int32)
    is_live = slot_order < tile_count[0, 0]
    earlier = (
        (owner_index[:, None] == owner_index[None, :])
        & is_live[None, :]
        & (slot_order[None, :] < slot_order[:, None])
    )
    slot_rank = jnp.sum(earlier.astype(jnp.int32), axis=1)
    slot_place = jnp.where(is_live, owner_index * CAP + slot_rank, grid_rows * columns * CAP)
    return slot_place, target


def collect_kernel(local_cols, land_ref, table_ref, tiles_ref, out_ref, pack_ref):
    out_ref[...] = jnp.zeros_like(out_ref)

    def step(n, carry):
        place = land_ref[n] - 1
        b = lax.rem(place, local_cols)

        @pl.when((place >= 0) & (b < NPANEL))
        def _():
            a = place // local_cols
            out_ref[b, a] = out_ref[b, a] + tiles_ref[n]

        return carry

    lax.fori_loop(0, land_ref.shape[0], step, 0)
    pack_ref[...] = jnp.zeros_like(pack_ref)

    def pack(n, carry):
        slot = table_ref[n]

        @pl.when((slot >= 0) & (slot < PACK))
        def _():
            part = PACK // PACK_PARTS
            pack_ref[slot // part, lax.rem(slot, part)] = out_ref[lax.rem(n, NPANEL), n // NPANEL]

        return carry

    lax.fori_loop(0, table_ref.shape[0], pack, 0)


def exchange_kernel(
    p_ref, s_ref, z_ref,
    g_recv, up_send, down_send,
    h_recv, x_send, y_send, core_send,
    z_send, z_recv,
):
    x = lax.axis_index("sib")
    r = lax.axis_index("row")
    z = lax.axis_index("col")
    last = lax.axis_size("col") - 1
    y, core = r // 2, lax.rem(r, 2)
    right_core = core == lax.rem(z, 2)
    is_source = right_core & (y == z // 2)
    is_relay = right_core & (y != z // 2)
    up, down = (x, r, z + 1), (x, r, z - 1)
    x_peer = (1 - x, r, z)
    y_peer = (x, lax.rem(r + 2, 4), z)
    core_peer = (x, r + 1 - 2 * core, z)
    has_up, has_down = z < last, z > 0

    def remote(src, dst, send, recv, device):
        return pltpu.make_async_remote_copy(
            src_ref=src, dst_ref=dst, send_sem=send, recv_sem=recv,
            device_id=device, device_id_type=pl.DeviceIdType.MESH,
        )

    barrier = pltpu.get_barrier_semaphore()
    for peer in (x_peer, y_peer, core_peer):
        pl.semaphore_signal(barrier, inc=1, device_id=peer, device_id_type=pl.DeviceIdType.MESH)

    @pl.when(has_up)
    def _():
        pl.semaphore_signal(barrier, inc=1, device_id=up, device_id_type=pl.DeviceIdType.MESH)

    @pl.when(has_down)
    def _():
        pl.semaphore_signal(barrier, inc=1, device_id=down, device_id_type=pl.DeviceIdType.MESH)

    pl.semaphore_wait(barrier, 3 + jnp.where(has_up, 1, 0) + jnp.where(has_down, 1, 0))

    def up_copy(src, c, p):
        return remote(src, s_ref.at[0, c, p], up_send.at[c, p], g_recv.at[c, p], up)

    def down_copy(src, c, p):
        return remote(src, s_ref.at[0, c, p], down_send.at[c, p], g_recv.at[c, p], down)

    def plane_copies(src, c, p):
        there = s_ref.at[1 + x, c, p]
        recv = h_recv.at[x, c, p]
        return (
            remote(src, there, x_send.at[c, p], recv, x_peer),
            remote(src, there, y_send.at[c, p], recv, y_peer),
            remote(src, there, core_send.at[x, c, p], recv, core_peer),
        )

    def relay_x(c, p):
        here = s_ref.at[1 + x, c, p]
        return remote(here, here, x_send.at[c, p], h_recv.at[x, c, p], x_peer)

    def to_core(k, c, p):
        here = s_ref.at[1 + k, c, p]
        return remote(here, here, core_send.at[k, c, p], h_recv.at[k, c, p], core_peer)

    def units(t):
        if t == 0:
            return [(z, None, 0)]
        return [(z - t, z >= t, -1), (z + t, z + t <= last, 1)]

    def guarded(condition, body):
        if condition is None:
            body()
        else:
            pl.when(condition)(body)

    def gather_step(p, t):
        for c, exists, side in units(t):
            def body(c=c, side=side):
                if side == 0:
                    src = p_ref.at[p]
                else:
                    src = s_ref.at[0, c, p]
                    up_copy(src, c, p).wait_recv()
                if side <= 0:
                    pl.when(has_up)(lambda: up_copy(src, c, p).start())
                if side >= 0:
                    pl.when(has_down)(lambda: down_copy(src, c, p).start())

                @pl.when(is_source)
                def _():
                    for copy in plane_copies(src, c, p):
                        copy.start()

                if side == 0:
                    s_ref[0, z, p] = p_ref[p]

            guarded(exists, body)

    def relay_step(p, t):
        for c, exists, side in units(t):
            def body(c=c):
                @pl.when(is_relay)
                def _():
                    to_core(x, c, p).wait_recv()
                    relay_x(c, p).start()
                    to_core(x, c, p).start()

                @pl.when(right_core)
                def _():
                    to_core(1 - x, c, p).wait_recv()
                    to_core(1 - x, c, p).start()

            guarded(exists, body)

    def corner_x():
        return remote(s_ref.at[0, :, 0, 0], z_ref.at[r], z_send.at[0], z_recv.at[0], x_peer)

    def corner_core():
        return remote(z_ref.at[r], z_ref.at[r], z_send.at[1], z_recv.at[1], core_peer)

    def corner_y():
        pair = z_ref.at[pl.ds(2 * y, 2)]
        return remote(pair, pair, z_send.at[2], z_recv.at[2], y_peer)

    def corner_first():
        @pl.when(x == 1)
        def _():
            corner_x().start()
            z_ref[r] = s_ref[0, :, 0, 0]

    def corner_second():
        @pl.when(x == 0)
        def _():
            corner_x().wait_recv()

        corner_core().start()

    def corner_third():
        corner_core().wait_recv()
        corner_y().start()

    corner_steps = [corner_first, corner_second, corner_third]
    steps = [(p, t) for p in range(p_ref.shape[0]) for t in range(4)]
    for n, (p, t) in enumerate(steps):
        gather_step(p, t)
        if n >= 3 and corner_steps:
            corner_steps.pop(0)()
        if n:
            relay_step(*steps[n - 1])
    relay_step(*steps[-1])
    for corner_step in corner_steps:
        corner_step()

    corner_y().wait_recv()
    pl.when(x == 1)(lambda: corner_x().wait_send())
    corner_core().wait_send()
    corner_y().wait_send()
    for p, t in steps:
        for c, exists, side in units(t):
            def body(c=c, side=side, p=p):
                src = p_ref.at[p] if side == 0 else s_ref.at[0, c, p]
                if side <= 0:
                    pl.when(has_up)(lambda: up_copy(src, c, p).wait_send())
                if side >= 0:
                    pl.when(has_down)(lambda: down_copy(src, c, p).wait_send())

                @pl.when(is_source)
                def _():
                    for copy in plane_copies(src, c, p):
                        copy.wait_send()

                @pl.when(is_relay)
                def _():
                    relay_x(c, p).wait_send()
                    to_core(x, c, p).wait_send()

                @pl.when(right_core)
                def _():
                    to_core(1 - x, c, p).wait_send()

                @pl.when(jnp.logical_not(right_core))
                def _():
                    to_core(x, c, p).wait_recv()
                    to_core(1 - x, c, p).wait_recv()

            guarded(exists, body)


def split(value):
    high = value.astype(jnp.bfloat16)
    return high, (value - high.astype(jnp.float32)).astype(jnp.bfloat16)


def dot3(left, right):
    dims = (((1,), (1,)), ((), ()))
    dot = functools.partial(lax.dot_general, dimension_numbers=dims, preferred_element_type=jnp.float32)
    return dot(left[0], right[0]) + (dot(left[0], right[1]) + dot(left[1], right[0]))


def front_kernel(local_cols, packed, where_ref, land_ref, *refs):
    if packed:
        table_ref, packs_ref, *refs = refs
    else:
        r_ref, c0_ref, c1_ref, *refs = refs
    z_ref, w_ref, tiles_ref, out_ref, wh, wl, qh, ql, pend, lh, ll, prod, count, place, head, link = refs
    step = pl.program_id(0)
    local_rows = out_ref.shape[0]
    b_block = out_ref.shape[1]
    group = 4
    solve_steps = 1 if packed else local_rows

    @pl.when(step == 0)
    def _():
        for p in range(NPANEL):
            wh[p], wl[p] = split(w_ref[p])
        corner = jnp.concatenate([z_ref[:, c].reshape(PANEL, TILE) for c in range(4)], axis=1)
        qh[...], ql[...] = split(dot3(split(corner), (wh[0], wl[0])))
        for n in range(5):
            count[n] = 0

        def clear(b, carry):
            head[b] = -1
            return carry

        lax.fori_loop(0, local_cols, clear, 0)

        def chain(n, carry):
            spot = land_ref[n] - 1

            @pl.when(spot >= 0)
            def _():
                b = lax.rem(spot, local_cols)
                link[n] = head[b]
                head[b] = n

            return carry

        lax.fori_loop(0, land_ref.shape[0], chain, 0)

    def solve(kind, done):
        base = jnp.where(kind == 0, 0, group + group * lax.rem(done, 2))
        chunk = kind * (local_rows // group) + done
        block = pend[pl.ds(base, group)].reshape(group * TILE, NPANEL * PANEL)
        first = dot3(split(block[:, :PANEL]), (wh[0], wl[0]))
        first_parts = split(first)
        rest = block[:, PANEL:] - dot3(first_parts, (qh[...], ql[...]))
        second = dot3(split(rest), (wh[1], wl[1]))
        kept = []
        for m in range(group):
            spot = place[kind, done * group + m]
            tile_row = jnp.where(kind == 0, spot * 8 + where_ref[0], spot * 4 + where_ref[1])
            kept.append(jnp.where(tile_row >= 8, second[m * TILE : (m + 1) * TILE], 0.0))
        second_parts = split(jnp.concatenate(kept, axis=0))
        lh[chunk, :, :PANEL], ll[chunk, :, :PANEL] = first_parts
        lh[chunk, :, PANEL:], ll[chunk, :, PANEL:] = second_parts

    def take(a):
        for kind, slab in ((0, 0), (1, 1), (1, 2)):
            if packed:
                spots = [
                    [table_ref[((slab * 4 + c) * local_rows + a) * NPANEL + p] for c in range(4)]
                    for p in range(NPANEL)
                ]
                largest = functools.reduce(jnp.maximum, spots[0] + spots[1])
                is_live = largest >= 0
            else:
                ref = (r_ref, c0_ref, c1_ref)[slab]
                is_live = jnp.max(jnp.abs(ref[...].reshape(-1, TILE))) > 0

            @pl.when(is_live & (a * 8 + where_ref[slab] >= 4))
            def _():
                n = count[kind]
                slot = lax.rem(n, group) if kind == 0 else group + lax.rem(n, 2 * group)
                for p in range(NPANEL):
                    for c in range(4):
                        start = p * PANEL + c * TILE
                        if packed:
                            spot = spots[p][c]
                            slot_of = jnp.maximum(spot, 0)
                            part = packs_ref.shape[3]
                            tile = packs_ref[
                                where_ref[4 + slab], c, slot_of // part, lax.rem(slot_of, part)
                            ]
                            tile = jnp.where(spot >= 0, tile, 0.0)
                        else:
                            tile = ref[0, c, p, 0]
                        pend[slot, :, start : start + TILE] = tile
                place[kind, n] = a if kind == 0 else 2 * a + slab - 1
                count[kind] = n + 1

        def flush(q, carry):
            kind, partial = q // 2, lax.rem(q, 2)
            n, done = count[kind], count[2 + kind]
            full = n >= group * done + group
            left_over = (a == local_rows - 1) & (n > group * done)

            @pl.when(((partial == 0) & full) | ((partial == 1) & left_over))
            def _():
                solve(kind, done)
                count[2 + kind] = done + 1

            return carry

        lax.fori_loop(0, 4, flush, 0)

    @pl.when(step < solve_steps)
    def _():
        if packed:
            def take_one(a, carry):
                take(a)
                return carry

            lax.fori_loop(0, local_rows, take_one, 0)
        else:
            take(step)

    @pl.when(step >= solve_steps)
    def _():
        b0 = (step - solve_steps) * b_block
        live_rows = count[0]
        out_ref[...] = jnp.zeros_like(out_ref)
        for k in range(b_block):
            n = count[4]

            @pl.when((n < count[1]) & (place[1, n] == b0 + k))
            def _():
                @pl.when(lax.rem(n, group) == 0)
                def _():
                    column = local_rows // group + n // group

                    def multiply(i, carry):
                        prod[i] = -dot3((lh[i], ll[i]), (lh[column], ll[column]))
                        return carry

                    lax.fori_loop(0, count[2], multiply, 0)

                lane = pl.multiple_of(lax.rem(n, group) * TILE, TILE)

                def put(i, carry):
                    row = pl.multiple_of(lax.rem(i, group) * TILE, TILE)
                    out_ref[place[0, i], k] = prod[i // group, pl.ds(row, TILE), pl.ds(lane, TILE)]
                    return carry

                lax.fori_loop(0, live_rows, put, 0)
                count[4] = n + 1

            def add(n):
                a = (land_ref[n] - 1) // local_cols
                out_ref[a, k] = out_ref[a, k] + tiles_ref[n]
                return link[n]

            lax.while_loop(lambda n: n >= 0, add, head[b0 + k])

        @pl.when(b0 == 0)
        def _():
            def replace(i, carry):
                a = place[0, i]
                row = pl.multiple_of(lax.rem(i, group) * TILE, TILE)
                for p in range(NPANEL):
                    @pl.when(a * 8 + where_ref[0] >= (p + 1) * 4)
                    def _():
                        lane = pl.multiple_of(p * PANEL + where_ref[1] * TILE, TILE)
                        at = (i // group, pl.ds(row, TILE), pl.ds(lane, TILE))
                        out_ref[a, p] = lh[at].astype(jnp.float32) + ll[at].astype(jnp.float32)

                return carry

            lax.fori_loop(0, live_rows, replace, 0)


def local_fast(child_tiles, child_rows, child_slots, tile_count, inverses):
    grid_rows = lax.axis_size("sib") * lax.axis_size("row")
    columns = lax.axis_size("col")
    devices = grid_rows * columns
    tile_order = NF // TILE
    local_rows = tile_order // grid_rows
    local_cols = tile_order // columns
    axes = ("sib", "row", "col")
    slot_place, target = route(child_rows, child_slots, tile_count, grid_rows, columns, local_cols)
    outgoing = (
        jnp.zeros((devices * CAP, TILE, TILE), jnp.float32)
        .at[slot_place]
        .set(child_tiles[0, 0], mode="drop")
    )
    places = local_rows * local_cols
    codes = lax.all_gather(slot_place * places + target, axes, axis=0, tiled=False)
    outgoing, codes = lax.optimization_barrier((outgoing, codes))
    arrived = lax.all_to_all(
        outgoing.reshape(devices, CAP, TILE, TILE), axes, split_axis=0, concat_axis=0, tiled=True
    ).reshape(devices * CAP, TILE, TILE)
    all_slot_places, all_targets = codes // places, codes % places
    my_places = lax.axis_index(axes) * CAP + jnp.arange(CAP, dtype=jnp.int32)
    landing = jnp.sum(
        jnp.where(
            all_slot_places[:, :, None] == my_places[None, None, :], all_targets[:, :, None] + 1, 0
        ),
        axis=1,
    ).reshape(devices * CAP)

    vmem = pl.BlockSpec(memory_space=pltpu.VMEM)
    smem = pl.BlockSpec(memory_space=pltpu.SMEM)
    panel_places = local_rows * NPANEL
    column = all_targets % local_cols
    key = jnp.where(
        (all_slot_places < devices * CAP) & (column < NPANEL),
        all_slot_places // CAP * panel_places + all_targets // local_cols * NPANEL + column,
        -1,
    ).reshape(-1)
    every_key = jnp.arange(devices * panel_places, dtype=jnp.int32)
    is_live = jnp.any(key[None, :] == every_key[:, None], axis=1).reshape(devices, panel_places)
    order_in = jnp.arange(panel_places, dtype=jnp.int32)
    is_live = is_live | (order_in[None, :] == 0)
    before = (order_in[None, :] < order_in[:, None])[None] & is_live[:, None, :]
    tables = jnp.where(is_live, jnp.sum(before.astype(jnp.int32), axis=2), -1)
    table = lax.dynamic_index_in_dim(tables, lax.axis_index(axes), 0, False)
    fits = jnp.max(tables) < PACK

    panels, pack = pl.pallas_call(
        functools.partial(collect_kernel, local_cols),
        out_shape=(
            jax.ShapeDtypeStruct((NPANEL, local_rows, TILE, TILE), jnp.float32),
            jax.ShapeDtypeStruct((PACK_PARTS, PACK // PACK_PARTS, TILE, TILE), jnp.float32),
        ),
        in_specs=[smem, smem, vmem],
        out_specs=(vmem, vmem),
        compiler_params=pltpu.CompilerParams(vmem_limit_bytes=24 * 2**20),
        name="collect",
    )(landing, table, arrived)

    my_sib = lax.axis_index("sib")
    my_row = lax.axis_index(("sib", "row"))
    my_col = lax.axis_index("col")
    is_source = lax.axis_index("row") == my_col
    picks = [jnp.where(is_source & (my_sib == k), 0, 1 + k) for k in range(2)]
    where = jnp.stack([my_row, my_col, my_col + 4, my_col, 0 * my_col, *picks]).astype(jnp.int32)
    by_grid_row = tables.reshape(grid_rows, columns * local_rows * NPANEL)
    slab_tables = jnp.concatenate(
        [lax.dynamic_index_in_dim(by_grid_row, g, 0, False) for g in (my_row, my_col, my_col + 4)]
    )

    dma = pltpu.SemaphoreType.DMA

    def exchange(block, collective_id, name):
        unit = (columns, block.shape[0])
        return pl.pallas_call(
            exchange_kernel,
            out_shape=(
                jax.ShapeDtypeStruct((3, columns, *block.shape), jnp.float32),
                jax.ShapeDtypeStruct((4, columns, TILE, TILE), jnp.float32),
            ),
            in_specs=[vmem],
            out_specs=(vmem, vmem),
            scratch_shapes=[
                dma(unit), dma(unit), dma(unit),
                dma((2,) + unit), dma(unit), dma(unit), dma((2,) + unit),
                dma((3,)), dma((3,)),
            ],
            compiler_params=pltpu.CompilerParams(
                collective_id=collective_id, has_side_effects=True, vmem_limit_bytes=40 * 2**20
            ),
            name=name,
        )(block)

    b_block = 2
    order = NPANEL * PANEL
    group = 4
    last = local_rows - 1

    def slab_spec(slab):
        return pl.BlockSpec(
            (1, columns, NPANEL, 1, TILE, TILE),
            lambda j, w, l: (w[4 + slab], 0, 0, jnp.minimum(j, last), 0, 0),
        )

    def whole(*shape):
        return pl.BlockSpec(shape, lambda j, w, l: (0,) * len(shape), pipeline_mode=pl.Buffered(1))

    def finish(packed, slab_specs, slab_args, corner, name):
        solve_steps = 1 if packed else local_rows
        return pl.pallas_call(
            functools.partial(front_kernel, local_cols, packed),
            grid_spec=pltpu.PrefetchScalarGridSpec(
                num_scalar_prefetch=2,
                grid=(solve_steps + local_cols // b_block,),
                in_specs=[
                    *slab_specs,
                    whole(4, columns, TILE, TILE),
                    whole(NPANEL, PANEL, PANEL),
                    whole(devices * CAP, TILE, TILE),
                ],
                out_specs=pl.BlockSpec(
                    (local_rows, b_block, TILE, TILE),
                    lambda j, w, l: (0, jnp.maximum(j - solve_steps, 0), 0, 0),
                ),
                scratch_shapes=[
                    pltpu.VMEM((NPANEL, PANEL, PANEL), jnp.bfloat16),
                    pltpu.VMEM((NPANEL, PANEL, PANEL), jnp.bfloat16),
                    pltpu.VMEM((PANEL, PANEL), jnp.bfloat16),
                    pltpu.VMEM((PANEL, PANEL), jnp.bfloat16),
                    pltpu.VMEM((3 * group, TILE, order), jnp.float32),
                    pltpu.VMEM(((local_rows + local_cols) // group, group * TILE, order), jnp.bfloat16),
                    pltpu.VMEM(((local_rows + local_cols) // group, group * TILE, order), jnp.bfloat16),
                    pltpu.VMEM((local_rows // group, group * TILE, group * TILE), jnp.float32),
                    pltpu.SMEM((8,), jnp.int32),
                    pltpu.SMEM((2, local_cols + group), jnp.int32),
                    pltpu.SMEM((local_cols,), jnp.int32),
                    pltpu.SMEM((devices * CAP,), jnp.int32),
                ],
            ),
            out_shape=jax.ShapeDtypeStruct((local_rows, local_cols, TILE, TILE), jnp.float32),
            compiler_params=pltpu.CompilerParams(vmem_limit_bytes=62 * 2**20),
            name=name,
        )(where, landing, *slab_args, corner, inverses, arrived)

    def by_packs():
        packs, corner = exchange(pack, 1, "exchange_packs")
        specs = [smem, whole(3, columns, PACK_PARTS, PACK // PACK_PARTS, TILE, TILE)]
        return finish(True, specs, [slab_tables, packs], corner, "front_packs")

    def by_panels():
        slabs, corner = exchange(panels, 0, "exchange_panels")
        return finish(False, [slab_spec(k) for k in range(3)], [slabs] * 3, corner, "front_panels")

    front = lax.cond(fits, by_packs, by_panels)
    return front.reshape(local_rows, 1, local_cols, 1, TILE, TILE)


def solution(mesh):
    sizes = (mesh.shape["sib"], mesh.shape["row"], mesh.shape["col"])
    return jax.shard_map(
        local_fast if sizes == (2, 4, 4) else local,
        mesh=mesh,
        in_specs=(
            P("sib", ("row", "col"), None, None, None),
            P("sib", None),
            P("sib", ("row", "col"), None),
            P("sib", ("row", "col")),
            P(),
        ),
        out_specs=P(None, ("sib", "row"), None, "col", None, None),
        check_vma=False,
    )
```
